512 devices in a mesh: dp: 32 (over y, z_lo, core), tensor: 16 (over x, z_hi).
Axes of the slice: x: 4, y: 8, z: 8 (z_hi: 4, z_lo: 2; z = z_hi * 2 + z_lo), core: 2. Of those that a mesh axis runs over, the one named last changes fastest.
Arguments:
- inputs: bfloat16 [32, 384, 5120], P('dp', None, 'tensor'), may hold values from -6 to 6, as said below
- w_query: bfloat16 [5120, 4096], P('dp', 'tensor'), as said below
- w_key: bfloat16 [5120, 4096], P('dp', 'tensor'), as said below
- w_value: bfloat16 [5120, 4096], P('dp', 'tensor'), may hold values from -0.078125 to 0.078125
- tangent: bfloat16 [5120, 4096], P('dp', 'tensor'), as said below
- gain_query: float32 [4096], P('tensor'), may hold values from 0.3 to 3, as said below
- gain_key: float32 [4096], P('tensor'), may hold values from 0.1 to 1.9
Outputs:
- curvature: float32 [5120, 4096], P('dp', 'tensor')
The draws below stay inside these ranges and needn't reach their ends.
Inputs may be any that keep to these rules, and one draw needn't show every extreme that they name: Layer inputs of order one. `w_query`: entries of order one over the square root of 5120. `w_key`: entries of order one over the square root of 5120. `tangent`: entries of order one over the square root of 5120. `gain_query`: positive gains of order one.
All inputs are finite; a program needn't handle non-finite values.
Results may differ from the reference program's by a relative error of at most 0.03.
Values may be sent and summed in bfloat16 or wider, within the bound.
No kernel may reach another device: no remote copies, remote signals or barrier semaphores. Data moves between devices by JAX's collectives and lax.ppermute only.
A program may use at most 64 MiB of HBM per device.

```python
import math
import jax
import jax.numpy as jnp
from jax import lax

D = 5120
HD = 128
SEQ = 384
REPLICAS = 32
WIDE = 4096


def base_weight(key):
    return jax.random.truncated_normal(key, -5.0, 5.0, (D, WIDE), jnp.float32) / math.sqrt(D)


def query_base(key):
    return base_weight(jax.random.fold_in(key, 11))


def column_rise(low, high):
    place = jnp.arange(WIDE).astype(jnp.float32) / (WIDE - 1)
    return low * jnp.exp(place * math.log(high / low))


def draw_w_query(key, part):
    values = query_base(key)
    return values.astype(jnp.bfloat16)


def draw_w_key(key, part):
    key = jax.random.fold_in(key, 12)
    values = base_weight(key)
    return values.astype(jnp.bfloat16)


def draw_tangent(key, part):
    shared = query_base(key)
    key = jax.random.fold_in(key, 14)
    noise = base_weight(key)
    rise = column_rise(0.5, 2.0)
    values = rise[None, :] * shared + 0.5 * noise
    return values.astype(jnp.bfloat16)


def draw_gain_query(key, part):
    key = jax.random.fold_in(key, 15)
    jitter = jax.random.uniform(key, (WIDE,), jnp.float32, -0.15, 0.15)
    rise = column_rise(0.6, 1.8)
    return rise * (1.0 + jitter)


def draw_inputs(key, part):
    key = jax.random.fold_in(key, 13)
    key_noise = jax.random.fold_in(key, 0)
    values = jax.random.truncated_normal(key_noise, -4.5, 4.5, (REPLICAS, SEQ, D), jnp.float32)
    return values.astype(jnp.bfloat16)


def block_scale(stream_key, extent, pieces, low, top_value):
    def one(dim, shards_of):
        steps = jax.random.uniform(jax.random.fold_in(jax.random.fold_in(stream_key, 6), dim), (shards_of,), jnp.float32, low / len(pieces), top_value / len(pieces))
        return jnp.repeat(jnp.exp(steps), extent[dim] // shards_of).reshape((-1,) + (1,) * (len(extent) - dim - 1))

    gain = one(*pieces[0])
    for cut in pieces[1:]:
        gain = gain * one(*cut)
    return gain


def bell_draw(stream_key, dims, spread, bound, cuts=(), held_as=jnp.bfloat16):
    loudness = block_scale(stream_key, dims, cuts, -0.22, 0.18) if cuts else 1.0
    values = jax.random.normal(stream_key, dims, jnp.float32) * spread * loudness
    return jnp.minimum(jnp.maximum(values, -bound), bound).astype(held_as)


def setup_inputs(seed: int = 0) -> dict:
    splits = jax.random.split(jax.random.key(seed), 8)
    inputs = draw_inputs(jax.random.fold_in(splits[7], 71), 0)
    w_query = draw_w_query(jax.random.fold_in(splits[7], 71), 0)
    w_key = draw_w_key(jax.random.fold_in(splits[7], 71), 0)
    w_value = bell_draw(splits[3], (D, WIDE), D ** -0.5, 0.078125, ((0, 32), (1, 16)))
    tangent = draw_tangent(jax.random.fold_in(splits[7], 71), 0)
    gain_query = draw_gain_query(jax.random.fold_in(splits[7], 71), 0)
    gain_key = jnp.clip(1.0 + 0.18 * jax.random.normal(splits[6], (WIDE,), jnp.float32), 0.1, 1.9)
    return {"inputs": inputs, "w_query": w_query, "w_key": w_key, "w_value": w_value, "tangent": tangent, "gain_query": gain_query, "gain_key": gain_key}


EPS = 1e-06

def replica(x, w_query, w_key, w_value, tangent, gain_query, gain_key):
    length = x.shape[0]
    wide = w_query.shape[1]
    heads = wide // HD
    scale = 1.0 / HD ** 0.5
    query = jnp.dot(x, w_query, preferred_element_type=jnp.float32)
    key = jnp.dot(x, w_key, preferred_element_type=jnp.float32)
    dquery = jnp.dot(x, tangent, preferred_element_type=jnp.float32)
    value = jnp.dot(x, w_value, preferred_element_type=jnp.float32).astype(jnp.bfloat16)
    rq = lax.rsqrt(lax.optimization_barrier(jnp.mean(query * query, axis=1, keepdims=True)) + EPS)
    rk = lax.rsqrt(lax.optimization_barrier(jnp.mean(key * key, axis=1, keepdims=True)) + EPS)
    tq = lax.optimization_barrier(jnp.mean(query * dquery, axis=1, keepdims=True))
    qn = (gain_query * query * rq).astype(jnp.bfloat16)
    kn = (gain_key * key * rk).astype(jnp.bfloat16)
    dqn = (gain_query * rq * (dquery - query * rq * rq * tq)).astype(jnp.bfloat16)
    qh = qn.reshape(length, heads, HD).astype(jnp.float32)
    kh = kn.reshape(length, heads, HD).astype(jnp.float32)
    dh = dqn.reshape(length, heads, HD).astype(jnp.float32)
    vh = value.reshape(length, heads, HD).astype(jnp.float32)
    places = jnp.arange(length)
    causal = places[None, :] <= places[:, None]
    scores = jnp.einsum('qhd,khd->hqk', qh, kh) * scale
    scores = jnp.where(causal[None], scores, -jnp.inf)
    top = lax.optimization_barrier(jnp.max(scores, axis=2, keepdims=True))
    expo = jnp.exp(scores - top)
    probs = expo / lax.optimization_barrier(jnp.sum(expo, axis=2, keepdims=True))
    dscore = jnp.einsum('qhd,khd->hqk', dh, kh) * scale
    dprob = probs * (dscore - lax.optimization_barrier(jnp.sum(probs * dscore, axis=2, keepdims=True)))
    dpb = dprob.astype(jnp.bfloat16).astype(jnp.float32)
    upper = jnp.einsum('hqk,khd->qhd', dpb, vh).astype(jnp.bfloat16).astype(jnp.float32)
    gprob = jnp.einsum('qhd,khd->hqk', upper, vh)
    gscore = (probs * (gprob - lax.optimization_barrier(jnp.sum(probs * gprob, axis=2, keepdims=True)))).astype(jnp.bfloat16).astype(jnp.float32)
    gqn = (jnp.einsum('hqk,khd->qhd', gscore, kh) * scale).reshape(length, wide)
    weighted = gain_query * gqn
    tb = lax.optimization_barrier(jnp.mean(query * weighted, axis=1, keepdims=True))
    gq = (rq * weighted - query * rq * rq * rq * tb).astype(jnp.bfloat16)
    term = lax.dot_general(x, gq, (((0,), (0,)), ((), ())), preferred_element_type=jnp.float32)
    return term.astype(jnp.bfloat16).astype(jnp.float32)

def reference(inputs, w_query, w_key, w_value, tangent, gain_query, gain_key):

    def step(total, x):
        return (total + replica(x, w_query, w_key, w_value, tangent, gain_query, gain_key), None)
    start = jnp.zeros(w_query.shape, jnp.float32)
    total, unused = lax.scan(step, start, inputs)
    return total
```

```python
import functools

import jax
import jax.numpy as jnp
from jax import lax
from jax.experimental import pallas as pl
from jax.experimental.pallas import tpu as pltpu
from jax.sharding import Mesh, PartitionSpec as P

HEADS = 32
HD = 128
EPS = 1e-06
BF = jnp.bfloat16
F32 = jnp.float32
VMEM_LIMIT = 48 * 1024 * 1024


def shift(value, axis, by, size):
    return lax.ppermute(value, axis, [(i, (i + by) % size) for i in range(size)])


def ring(block, axis, size):
    half = block.shape[0] // 2
    up, down = [block], []
    low, high = block, block
    for _ in range(size // 2 - 1):
        low, high = shift(low, axis, 1, size), shift(high, axis, -1, size)
        up.append(low)
        down.append(high)
    up.append(shift(low[:half], axis, 1, size))
    down.append(shift(high[half:], axis, -1, size))
    return up + down[::-1]


def project_kernel(place, xt_hbm, mine, theirs, qkd, value, stats, xr, acc, sem, *, wide, rows, chunk):
    k = pl.program_id(0)
    steps = pl.num_programs(0)
    half = steps // 2
    y, zl, c = place[0], place[1], place[2]

    @pl.when(k == 0)
    def _():
        for side in range(2):
            for i in range(8):
                for j in range(2):
                    source = lax.rem(y + 8 - i, 8) * 4 + lax.rem(zl + j, 2) * 2 + lax.rem(c + side, 2)
                    pltpu.make_async_copy(
                        xt_hbm.at[pl.ds(pl.multiple_of(source * rows, rows), rows), :],
                        xr.at[pl.ds((side * 16 + i * 2 + j) * rows, rows), :],
                        sem,
                    ).start()
        acc[...] = jnp.zeros_like(acc)
        pltpu.make_async_copy(xt_hbm, xr, sem).wait()

    x = xr[pl.ds(pl.multiple_of(k * chunk, chunk), chunk), :]

    @pl.when(k < half)
    def _():
        acc[...] += lax.dot_general(x, mine[...], (((0,), (0,)), ((), ())), preferred_element_type=F32)

    @pl.when(k >= half)
    def _():
        acc[...] += lax.dot_general(x, theirs[...], (((0,), (0,)), ((), ())), preferred_element_type=F32)

    @pl.when(k == steps - 1)
    def _():
        q, key, dq = acc[:, :wide], acc[:, wide : 2 * wide], acc[:, 2 * wide : 3 * wide]
        qkd[...] = acc[:, : 3 * wide]
        value[...] = acc[:, 3 * wide :].astype(BF)
        lane = lax.broadcasted_iota(jnp.int32, (q.shape[0], 128), 1)
        sums = [jnp.sum(t, axis=1, keepdims=True) for t in (q * q, key * key, q * dq)]
        packed = jnp.where(lane == 0, sums[0], jnp.where(lane == 1, sums[1], jnp.where(lane == 2, sums[2], 0.0)))
        stats[...] = packed.T[:8]


def project(place, xt, mine, theirs, wide):
    length = xt.shape[1]
    depth = mine.shape[0]
    rows = xt.shape[0] // 32
    chunk = 512
    half = depth // chunk
    return pl.pallas_call(
        functools.partial(project_kernel, wide=wide, rows=rows, chunk=chunk),
        grid=(2 * half,),
        in_specs=[
            pl.BlockSpec(memory_space=pltpu.SMEM),
            pl.BlockSpec(memory_space=pl.ANY),
            pl.BlockSpec((chunk, 4 * wide), lambda k: (jnp.minimum(k, half - 1), 0)),
            pl.BlockSpec((chunk, 4 * wide), lambda k: (jnp.maximum(k - half, 0), 0)),
        ],
        out_specs=[
            pl.BlockSpec((length, 3 * wide), lambda k: (0, 0)),
            pl.BlockSpec((length, wide), lambda k: (0, 0)),
            pl.BlockSpec((8, length), lambda k: (0, 0)),
        ],
        out_shape=[
            jax.ShapeDtypeStruct((length, 3 * wide), F32),
            jax.ShapeDtypeStruct((length, wide), BF),
            jax.ShapeDtypeStruct((8, length), F32),
        ],
        scratch_shapes=[
            pltpu.VMEM(xt.shape, BF),
            pltpu.VMEM((length, 4 * wide), F32),
            pltpu.SemaphoreType.DMA,
        ],
        compiler_params=pltpu.CompilerParams(vmem_limit_bytes=VMEM_LIMIT),
        name="project",
    )(place, xt, mine, theirs)


def columns(sums):
    full = jnp.concatenate([sums, jnp.zeros((120, sums.shape[1]), F32)], axis=0)
    return full.T


def attend_kernel(sums, qkd, value, gains, weighted, stats, *, wide, total):
    length = qkd.shape[0]
    scale = 1.0 / HD**0.5
    cols = columns(sums[...])
    rq = lax.rsqrt(cols[:, 0:1] / total + EPS)
    rk = lax.rsqrt(cols[:, 1:2] / total + EPS)
    tq = cols[:, 2:3] / total
    causal = lax.broadcasted_iota(jnp.int32, (length, length), 1) <= lax.broadcasted_iota(
        jnp.int32, (length, length), 0
    )
    nt = (((1,), (1,)), ((), ()))
    back = jnp.zeros((length, 1), F32)
    for h in range(wide // HD):
        at = slice(h * HD, (h + 1) * HD)
        q = qkd[:, h * HD : (h + 1) * HD]
        key = qkd[:, wide + h * HD : wide + (h + 1) * HD]
        dq = qkd[:, 2 * wide + h * HD : 2 * wide + (h + 1) * HD]
        v = value[:, at]
        gq, gk = gains[0:1, at], gains[1:2, at]
        qn = (gq * q * rq).astype(BF)
        kn = (gk * key * rk).astype(BF)
        dqn = (gq * rq * (dq - q * rq * rq * tq)).astype(BF)
        scores = lax.dot_general(qn, kn, nt, preferred_element_type=F32) * scale
        scores = jnp.where(causal, scores, -jnp.inf)
        expo = jnp.exp(scores - jnp.max(scores, axis=1, keepdims=True))
        probs = expo / jnp.sum(expo, axis=1, keepdims=True)
        ds = lax.dot_general(dqn, kn, nt, preferred_element_type=F32) * scale
        dpb = (probs * (ds - jnp.sum(probs * ds, axis=1, keepdims=True))).astype(BF)
        upper = jnp.dot(dpb, v, preferred_element_type=F32).astype(BF)
        gp = lax.dot_general(upper, v, nt, preferred_element_type=F32)
        gs = (probs * (gp - jnp.sum(probs * gp, axis=1, keepdims=True))).astype(BF)
        w = gq * (jnp.dot(gs, kn, preferred_element_type=F32) * scale)
        weighted[:, at] = w
        back += jnp.sum(q * w, axis=1, keepdims=True)
    lane = lax.broadcasted_iota(jnp.int32, (length, 128), 1)
    stats[...] = jnp.where(lane == 0, back, 0.0).T[:8]


def attend(sums, qkd, value, gains, wide, total):
    length = qkd.shape[0]
    return pl.pallas_call(
        functools.partial(attend_kernel, wide=wide, total=total),
        out_shape=[
            jax.ShapeDtypeStruct((length, wide), F32),
            jax.ShapeDtypeStruct((8, length), F32),
        ],
        compiler_params=pltpu.CompilerParams(vmem_limit_bytes=VMEM_LIMIT),
        name="attend",
    )(sums, qkd, value, gains)


def outer_kernel(place, sums, back, q, weighted, xt, keep, send, gq, *, total, rows):
    c = place[2]

    @pl.when(pl.program_id(0) == 0)
    def _():
        rq = lax.rsqrt(columns(sums[...])[:, 0:1] / total + EPS)
        tb = columns(back[...])[:, 0:1] / total
        gq[...] = (rq * weighted[...] - q[...] * rq * rq * rq * tb).astype(BF)

    term = jnp.dot(xt[...], gq[...], preferred_element_type=F32)
    for i in range(term.shape[0] // (2 * rows)):
        first = term[2 * i * rows : (2 * i + 1) * rows]
        second = term[(2 * i + 1) * rows : (2 * i + 2) * rows]
        keep[i * rows : (i + 1) * rows, :] = jnp.where(c == 0, first, second)
        send[i * rows : (i + 1) * rows, :] = jnp.where(c == 0, second, first).astype(BF)


def outer(place, sums, back, qkd, weighted, xt, total):
    depth, length = xt.shape
    wide = weighted.shape[1]
    steps = 4
    block = depth // steps
    return pl.pallas_call(
        functools.partial(outer_kernel, total=total, rows=depth // 32),
        grid=(steps,),
        in_specs=[
            pl.BlockSpec(memory_space=pltpu.SMEM),
            pl.BlockSpec((8, length), lambda k: (0, 0)),
            pl.BlockSpec((8, length), lambda k: (0, 0)),
            pl.BlockSpec((length, wide), lambda k: (0, 0)),
            pl.BlockSpec((length, wide), lambda k: (0, 0)),
            pl.BlockSpec((block, length), lambda k: (k, 0)),
        ],
        out_specs=[
            pl.BlockSpec((block // 2, wide), lambda k: (k, 0)),
            pl.BlockSpec((block // 2, wide), lambda k: (k, 0)),
        ],
        out_shape=[
            jax.ShapeDtypeStruct((depth // 2, wide), F32),
            jax.ShapeDtypeStruct((depth // 2, wide), BF),
        ],
        scratch_shapes=[pltpu.VMEM((length, wide), BF)],
        compiler_params=pltpu.CompilerParams(vmem_limit_bytes=VMEM_LIMIT),
        name="outer",
    )(place, sums, back, qkd, weighted, xt)


def sum_over_heads(stats, count):
    n = stats.shape[1]
    mine = stats[:count].reshape(1, count * n // 128, 128)
    got = lax.all_to_all(jnp.broadcast_to(mine, (16,) + mine.shape[1:]), ("x", "zh"), 0, 0, tiled=True)
    summed = jnp.sum(got, axis=0).reshape(count, n)
    return jnp.concatenate([summed, jnp.zeros((8 - count, n), F32)], axis=0)


def on_device(inputs, w_query, w_key, w_value, tangent, gain_query, gain_key):
    wide = w_query.shape[1]
    total = HEADS * HD
    place = jnp.stack([lax.axis_index("y"), lax.axis_index("zl"), lax.axis_index("c")]).astype(jnp.int32)

    weights = jnp.concatenate([w_query, w_key, tangent, w_value], axis=1)
    other = shift(weights, "zl", 1, 2)
    xt = lax.all_gather(inputs[0].T, "zh", axis=0, tiled=True)
    xt = lax.all_gather(xt, "x", axis=0, tiled=True)
    mine = jnp.concatenate(ring(jnp.concatenate([weights, other], axis=0), "y", 8), axis=0)
    theirs = shift(mine, "c", 1, 2)

    qkd, value, stats = project(place, xt, mine, theirs, wide)
    sums = sum_over_heads(stats, 3)
    gains = jnp.concatenate([gain_query[None], gain_key[None], jnp.zeros((6, wide), F32)], axis=0)
    weighted, stats = attend(sums, qkd, value, gains, wide, total)
    back = sum_over_heads(stats, 1)
    keep, send = outer(place, sums, back, qkd, weighted, xt, total)

    part = (keep + shift(send, "c", 1, 2).astype(F32)).astype(BF)
    got = lax.all_to_all(part.reshape(16, part.shape[0] // 16, wide), ("y", "zl"), 0, 0, tiled=True)
    return jnp.sum(got.astype(F32), axis=0)


def solution(mesh):
    fine = Mesh(mesh.devices.reshape(8, 2, 2, 4, 4), ("y", "zl", "c", "x", "zh"))
    dp, tensor = ("y", "zl", "c"), ("x", "zh")
    return jax.shard_map(
        on_device,
        mesh=fine,
        in_specs=(
            P(dp, None, tensor),
            P(dp, tensor),
            P(dp, tensor),
            P(dp, tensor),
            P(dp, tensor),
            P(tensor),
            P(tensor),
        ),
        out_specs=P(dp, tensor),
        check_vma=False,
    )
```

```python
import functools

import jax
import jax.numpy as jnp
from jax import lax
from jax.experimental import pallas as pl
from jax.experimental.pallas import tpu as pltpu
from jax.sharding import Mesh, PartitionSpec as P

HEADS = 32
HD = 128
EPS = 1e-06
BF = jnp.bfloat16
F32 = jnp.float32
Y = ("yh", "yl")
MIB = 1024 * 1024


def shift(value, axis, by, size):
    return lax.ppermute(value, axis, [(i, (i + by) % size) for i in range(size)])


def weight_ring(own, other):
    up, down = shift(own, Y, 1, 8), shift(own, Y, -1, 8)
    parts = [(own, 0, 4, 0, 0, 0), (other, 0, 4, 0, 1, 0), (up, 0, 4, 1, 0, 0), (down, 0, 4, 7, 0, 0)]
    up = shift(jnp.concatenate([up, other]), Y, 1, 8)
    down = shift(jnp.concatenate([other, down]), Y, -1, 8)
    parts += [(up, 0, 4, 2, 0, 0), (up, 4, 4, 1, 1, 0), (down, 0, 4, 7, 1, 0), (down, 4, 4, 6, 0, 0)]
    up, down = shift(up, Y, 1, 8), shift(down, Y, -1, 8)
    parts += [(up, 0, 4, 3, 0, 0), (up, 4, 4, 2, 1, 0), (down, 0, 4, 6, 1, 0), (down, 4, 4, 5, 0, 0)]
    up, down = shift(up[2:], Y, 1, 8), shift(down[:6], Y, -1, 8)
    parts += [(up, 0, 2, 4, 0, 2), (up, 2, 4, 3, 1, 0), (down, 0, 4, 5, 1, 0), (down, 4, 2, 4, 0, 0)]
    up, down = shift(up[4:], Y, 1, 8), shift(down[:2], Y, -1, 8)
    parts += [(up, 0, 2, 4, 1, 2), (down, 0, 2, 4, 1, 0)]
    return parts


def project_kernel(place, x_hbm, *refs, layout, which, wide, rows):
    count = max(entry[0] for entry in layout) + 1
    pieces = refs[:count]
    out, x, w, sem = refs[count:]
    length = out.shape[0]
    y, zl = place[0], place[1]
    groups = sem.shape[0]
    span = x.shape[0] // groups
    spots = {}
    for _, _, _, back, step, _ in layout:
        spots.setdefault((back, step), len(spots))
    for (back, step), spot in spots.items():
        source = lax.rem(y + 8 - back, 8) * 2 + lax.rem(zl + step, 2)
        at = pl.ds(spot * rows, rows)
        group = spot * rows // span
        pltpu.make_async_copy(
            x_hbm.at[pl.ds(pl.multiple_of(source * rows, rows), rows), pl.ds(which * length, length)],
            x.at[at, :],
            sem.at[group, 0],
        ).start()
        for piece, first, entries, b, s, weight in layout:
            if (b, s) == (back, step):
                pltpu.make_async_copy(
                    pieces[piece].at[pl.ds(first, entries)], w.at[pl.ds(weight, entries), at, :], sem.at[group, 1]
                ).start()
    for g in range(groups):
        at = pl.ds(g * span, span)
        pltpu.make_async_copy(x.at[at, :], x.at[at, :], sem.at[g, 0]).wait()
        pltpu.make_async_copy(w.at[:, at, :], w.at[:, at, :], sem.at[g, 1]).wait()
        for i in range(4):
            part = lax.dot_general(x[at, :], w[i, at, :], (((0,), (0,)), ((), ())), preferred_element_type=F32)
            cols = slice(i * wide, (i + 1) * wide)
            out[:, cols] = part if g == 0 else out[:, cols] + part


def project(place, x, parts, which, wide):
    depth, length = x.shape[0], x.shape[1] // 2
    arrays = []
    layout = []
    for array, *rest in parts:
        known = [i for i, other in enumerate(arrays) if other is array]
        if not known:
            arrays.append(array)
        layout.append((known[0] if known else len(arrays) - 1, *rest))
    return pl.pallas_call(
        functools.partial(project_kernel, layout=tuple(layout), which=which, wide=wide, rows=depth // 16),
        in_specs=[pl.BlockSpec(memory_space=pltpu.SMEM)]
        + [pl.BlockSpec(memory_space=pl.ANY)] * (1 + len(arrays)),
        out_shape=jax.ShapeDtypeStruct((length, 4 * wide), F32),
        scratch_shapes=[
            pltpu.VMEM((depth, length), BF),
            pltpu.VMEM((4, depth, wide), BF),
            pltpu.SemaphoreType.DMA((4, 2)),
        ],
        compiler_params=pltpu.CompilerParams(vmem_limit_bytes=44 * MIB),
        cost_estimate=pl.CostEstimate(
            flops=2 * length * depth * 4 * wide, bytes_accessed=2 * depth * (length + 4 * wide), transcendentals=0
        ),
        name="project",
    )(place, x, *arrays)


def merge_kernel(one, two, qkd, value, stats, *, wide):
    whole = [one[:, i * wide : (i + 1) * wide] + two[:, i * wide : (i + 1) * wide] for i in range(4)]
    for i in range(3):
        qkd[:, i * wide : (i + 1) * wide] = whole[i]
    value[...] = whole[3].astype(BF)
    q, key, dq = whole[:3]
    lane = lax.broadcasted_iota(jnp.int32, (q.shape[0], 128), 1)
    sums = [jnp.sum(t, axis=1, keepdims=True) for t in (q * q, key * key, q * dq)]
    packed = jnp.where(lane == 0, sums[0], jnp.where(lane == 1, sums[1], jnp.where(lane == 2, sums[2], 0.0)))
    stats[...] = packed.T[:8]


def merge(one, two, wide):
    length = one.shape[0]
    return pl.pallas_call(
        functools.partial(merge_kernel, wide=wide),
        out_shape=[
            jax.ShapeDtypeStruct((length, 3 * wide), F32),
            jax.ShapeDtypeStruct((length, wide), BF),
            jax.ShapeDtypeStruct((8, length), F32),
        ],
        compiler_params=pltpu.CompilerParams(vmem_limit_bytes=16 * MIB),
        name="merge",
    )(one, two)


def columns(sums):
    full = jnp.concatenate([sums, jnp.zeros((128 - sums.shape[0], sums.shape[1]), F32)], axis=0)
    return full.T


def attend_kernel(sums, qkd, value, gains, weighted, stats, *, wide, total):
    length = qkd.shape[0]
    scale = 1.0 / HD**0.5
    cols = columns(sums[...])
    rq = lax.rsqrt(cols[:, 0:1] / total + EPS)
    rk = lax.rsqrt(cols[:, 1:2] / total + EPS)
    tq = cols[:, 2:3] / total
    causal = lax.broadcasted_iota(jnp.int32, (length, length), 1) <= lax.broadcasted_iota(
        jnp.int32, (length, length), 0
    )
    nt = (((1,), (1,)), ((), ()))
    back = jnp.zeros((length, 1), F32)
    for h in range(wide // HD):
        at = slice(h * HD, (h + 1) * HD)
        q = qkd[:, h * HD : (h + 1) * HD]
        key = qkd[:, wide + h * HD : wide + (h + 1) * HD]
        dq = qkd[:, 2 * wide + h * HD : 2 * wide + (h + 1) * HD]
        v = value[:, at]
        gq, gk = gains[0:1, at], gains[1:2, at]
        qn = (gq * q * rq).astype(BF)
        kn = (gk * key * rk).astype(BF)
        dqn = (gq * rq * (dq - q * rq * rq * tq)).astype(BF)
        scores = lax.dot_general(qn, kn, nt, preferred_element_type=F32) * scale
        scores = jnp.where(causal, scores, -jnp.inf)
        expo = jnp.exp(scores - jnp.max(scores, axis=1, keepdims=True))
        probs = expo / jnp.sum(expo, axis=1, keepdims=True)
        ds = lax.dot_general(dqn, kn, nt, preferred_element_type=F32) * scale
        dpb = (probs * (ds - jnp.sum(probs * ds, axis=1, keepdims=True))).astype(BF)
        upper = jnp.dot(dpb, v, preferred_element_type=F32).astype(BF)
        gp = lax.dot_general(upper, v, nt, preferred_element_type=F32)
        gs = (probs * (gp - jnp.sum(probs * gp, axis=1, keepdims=True))).astype(BF)
        w = gq * (jnp.dot(gs, kn, preferred_element_type=F32) * scale)
        weighted[:, at] = w
        back += jnp.sum(q * w, axis=1, keepdims=True)
    lane = lax.broadcasted_iota(jnp.int32, (length, 128), 1)
    stats[...] = jnp.where(lane == 0, back, 0.0).T[:8]


def attend(sums, qkd, value, gains, wide, total):
    length = qkd.shape[0]
    return pl.pallas_call(
        functools.partial(attend_kernel, wide=wide, total=total),
        out_shape=[
            jax.ShapeDtypeStruct((length, wide), F32),
            jax.ShapeDtypeStruct((8, length), F32),
        ],
        compiler_params=pltpu.CompilerParams(vmem_limit_bytes=16 * MIB),
        name="attend",
    )(sums, qkd, value, gains)


def grad_kernel(sums, back, qkd, weighted, gq, *, wide, total):
    rq = lax.rsqrt(columns(sums[...])[:, 0:1] / total + EPS)
    tb = columns(back[...])[:, 0:1] / total
    gq[...] = (rq * weighted[...] - qkd[:, :wide] * rq * rq * rq * tb).astype(BF)


def grad(sums, back, qkd, weighted, total):
    length, wide = weighted.shape
    return pl.pallas_call(
        functools.partial(grad_kernel, wide=wide, total=total),
        out_shape=jax.ShapeDtypeStruct((length, wide), BF),
        name="grad",
    )(sums, back, qkd, weighted)


def outer_kernel(place, x, near, gq, gq_core, gq_near, gq_near_core, term):
    length = gq.shape[0]
    for i in range(x.shape[0]):
        total = jnp.dot(x[i, 0, :, :length], gq[...], preferred_element_type=F32)
        total += jnp.dot(x[i, 0, :, length:], gq_core[...], preferred_element_type=F32)
        total += jnp.dot(near[i, :, :length], gq_near[...], preferred_element_type=F32)
        total += jnp.dot(near[i, :, length:], gq_near_core[...], preferred_element_type=F32)
        term[i] = total.astype(BF)


def outer(place, x, near, grads):
    _, _, rows, tokens = x.shape
    length, wide = grads[0].shape
    steps = 2
    block = 4 // steps
    return pl.pallas_call(
        outer_kernel,
        grid_spec=pltpu.PrefetchScalarGridSpec(
            num_scalar_prefetch=1,
            grid=(steps,),
            in_specs=[
                pl.BlockSpec((block, 1, rows, tokens), lambda k, place: (k, lax.rem(place[0], 2), 0, 0)),
                pl.BlockSpec((block, rows, tokens), lambda k, place: (k, 0, 0)),
            ]
            + [pl.BlockSpec((length, wide), lambda k, place: (0, 0))] * 4,
            out_specs=pl.BlockSpec((block, rows, wide), lambda k, place: (k, 0, 0)),
        ),
        out_shape=jax.ShapeDtypeStruct((4, rows, wide), BF),
        compiler_params=pltpu.CompilerParams(vmem_limit_bytes=20 * MIB),
        cost_estimate=pl.CostEstimate(
            flops=16 * rows * tokens * wide, bytes_accessed=16 * rows * tokens, transcendentals=0
        ),
        name="outer",
    )(place, x, near, *grads)


def sum_over_heads(stats, count):
    n = stats.shape[1]
    mine = stats[:count].reshape(1, count * n // 128, 128)
    got = lax.all_to_all(jnp.broadcast_to(mine, (16,) + mine.shape[1:]), ("x", "zh"), 0, 0, tiled=True)
    return jnp.sum(got, axis=0).reshape(count, n)


def on_device(inputs, w_query, w_key, w_value, tangent, gain_query, gain_key):
    wide = w_query.shape[1]
    total = HEADS * HD
    place = jnp.stack([lax.axis_index(Y), lax.axis_index("zl")]).astype(jnp.int32)
    core = lax.axis_index("c")
    tie = lax.optimization_barrier

    halves = inputs[0].T.reshape(2, inputs.shape[2] // 2, inputs.shape[1])
    kept = lax.dynamic_index_in_dim(halves, core, 0, keepdims=False)
    given = lax.dynamic_index_in_dim(halves, 1 - core, 0, keepdims=False)
    x = jnp.concatenate([kept, shift(given, "c", 1, 2)], axis=1)
    x = lax.all_gather(x, ("x", "zh"), axis=0, tiled=True)

    weights = jnp.stack([w_query, w_key, tangent, w_value])
    parts = weight_ring(weights, shift(weights, "zl", 1, 2))
    x, *last = tie((x, parts[-1][0], parts[-2][0]))
    parts[-1], parts[-2] = (last[0], *parts[-1][1:]), (last[1], *parts[-2][1:])

    theirs = project(place, x, parts, 1, wide)
    x, theirs = tie((x, theirs))
    fine = x.reshape(4, 2, x.shape[0] // 8, x.shape[1])
    theirs = shift(theirs, "c", 1, 2)
    near = shift(lax.dynamic_index_in_dim(fine, 1 - lax.axis_index("yl"), 1, keepdims=False), "yl", 1, 2)
    qkd, value, stats = merge(project(place, x, parts, 0, wide), theirs, wide)
    sums = sum_over_heads(stats, 3)
    weighted, stats = attend(sums, qkd, value, jnp.stack([gain_query, gain_key]), wide, total)
    back = sum_over_heads(stats, 1)
    gq = grad(sums, back, qkd, weighted, total)

    gq_near = shift(gq, "yl", 1, 2)
    gq_core = shift(gq, "c", 1, 2)
    term = outer(place, fine, near, (gq, gq_core, gq_near, shift(gq_near, "c", 1, 2)))
    got = lax.all_to_all(term.reshape(8, -1, wide), ("yh", "zl"), 0, 0, tiled=True)
    return jnp.sum(got.astype(F32), axis=0)


def solution(mesh):
    fine = Mesh(mesh.devices.reshape(4, 2, 2, 2, 4, 4), ("yh", "yl", "zl", "c", "x", "zh"))
    dp, tensor = ("yh", "yl", "zl", "c"), ("x", "zh")
    return jax.shard_map(
        on_device,
        mesh=fine,
        in_specs=(
            P(dp, None, tensor),
            P(dp, tensor),
            P(dp, tensor),
            P(dp, tensor),
            P(dp, tensor),
            P(tensor),
            P(tensor),
        ),
        out_specs=P(dp, tensor),
        check_vma=False,
    )
```

```python
import functools

import jax
import jax.numpy as jnp
from jax import lax
from jax.experimental import pallas as pl
from jax.experimental.pallas import tpu as pltpu
from jax.sharding import Mesh, PartitionSpec as P

HEADS = 32
HD = 128
EPS = 1e-06
BF = jnp.bfloat16
F32 = jnp.float32
Y = ("yh", "yl")
MIB = 1024 * 1024


def shift(value, axis, by, size):
    return lax.ppermute(value, axis, [(i, (i + by) % size) for i in range(size)])


def weight_ring(own, other):
    up, down = shift(own, Y, 1, 8), shift(own, Y, -1, 8)
    parts = [(own, 0, 4, 0, 0, 0), (other, 0, 4, 0, 1, 0), (up, 0, 4, 1, 0, 0), (down, 0, 4, 7, 0, 0)]
    up = shift(jnp.concatenate([up, other]), Y, 1, 8)
    down = shift(jnp.concatenate([other, down]), Y, -1, 8)
    parts += [(up, 0, 4, 2, 0, 0), (up, 4, 4, 1, 1, 0), (down, 0, 4, 7, 1, 0), (down, 4, 4, 6, 0, 0)]
    up, down = shift(up, Y, 1, 8), shift(down, Y, -1, 8)
    parts += [(up, 0, 4, 3, 0, 0), (up, 4, 4, 2, 1, 0), (down, 0, 4, 6, 1, 0), (down, 4, 4, 5, 0, 0)]
    up, down = shift(up[2:], Y, 1, 8), shift(down[:6], Y, -1, 8)
    parts += [(up, 0, 2, 4, 0, 2), (up, 2, 4, 3, 1, 0), (down, 0, 4, 5, 1, 0), (down, 4, 2, 4, 0, 0)]
    up, down = shift(up[4:], Y, 1, 8), shift(down[:2], Y, -1, 8)
    parts += [(up, 0, 2, 4, 1, 2), (down, 0, 2, 4, 1, 0)]
    return parts


def project_kernel(place, x_hbm, *refs, layout, wide, rows):
    count = max(entry[0] for entry in layout) + 1
    pieces = refs[:count]
    own, theirs, near, x, w, sem, out_sem = refs[count:]
    length = own.shape[0]
    y, zl = place[0], place[1]
    groups = sem.shape[0]
    span = x.shape[0] // groups
    spots = {}
    for _, _, _, back, step, _ in layout:
        spots.setdefault((back, step), len(spots))

    def source(back, step):
        return lax.rem(y + 8 - back, 8), lax.rem(zl + step, 2)

    def block(index):
        return pl.ds(pl.multiple_of(index * rows, rows), rows)

    for (back, step), spot in spots.items():
        far_y, far_zl = source(back, step)
        at = pl.ds(spot * rows, rows)
        group = spot * rows // span
        index = (lax.rem(far_y, 2) * 2 + far_zl) * 4 + lax.div(far_y, 2)
        pltpu.make_async_copy(x_hbm.at[block(index), :], x.at[at, :], sem.at[group, 0]).start()
        for piece, first, entries, b, s, weight in layout:
            if (b, s) == (back, step):
                pltpu.make_async_copy(
                    pieces[piece].at[pl.ds(first, entries)], w.at[pl.ds(weight, entries), at, :], sem.at[group, 1]
                ).start()
    for g in range(groups):
        at = pl.ds(g * span, span)
        pltpu.make_async_copy(x.at[at, :], x.at[at, :], sem.at[g, 0]).wait()
        for (back, step), spot in spots.items():
            if back % 2 and spot * rows // span == g:
                far_y, far_zl = source(back, step)
                pltpu.make_async_copy(
                    x.at[pl.ds(spot * rows, rows), :], near.at[block(far_zl * 4 + lax.div(far_y, 2)), :], out_sem
                ).start()
        pltpu.make_async_copy(w.at[:, at, :], w.at[:, at, :], sem.at[g, 1]).wait()
        for i in range(4):
            part = lax.dot_general(x[at, :], w[i, at, :], (((0,), (0,)), ((), ())), preferred_element_type=F32)
            cols = slice(i * wide, (i + 1) * wide)
            own[:, cols] = part[:length] if g == 0 else own[:, cols] + part[:length]
            theirs[:, cols] = part[length:] if g == 0 else theirs[:, cols] + part[length:]
    pltpu.make_async_copy(near, near, out_sem).wait()


def project(place, x, parts, wide):
    depth, length = x.shape[0], x.shape[1] // 2
    arrays = []
    layout = []
    for array, *rest in parts:
        known = [i for i, other in enumerate(arrays) if other is array]
        if not known:
            arrays.append(array)
        layout.append((known[0] if known else len(arrays) - 1, *rest))
    return pl.pallas_call(
        functools.partial(project_kernel, layout=tuple(layout), wide=wide, rows=depth // 16),
        in_specs=[pl.BlockSpec(memory_space=pltpu.SMEM)]
        + [pl.BlockSpec(memory_space=pl.ANY)] * (1 + len(arrays)),
        out_specs=[
            pl.BlockSpec(memory_space=pltpu.VMEM),
            pl.BlockSpec(memory_space=pltpu.VMEM),
            pl.BlockSpec(memory_space=pl.ANY),
        ],
        out_shape=[
            jax.ShapeDtypeStruct((length, 4 * wide), F32),
            jax.ShapeDtypeStruct((length, 4 * wide), F32),
            jax.ShapeDtypeStruct((depth // 2, 2 * length), BF),
        ],
        scratch_shapes=[
            pltpu.VMEM(x.shape, BF),
            pltpu.VMEM((4, depth, wide), BF),
            pltpu.SemaphoreType.DMA((2, 2)),
            pltpu.SemaphoreType.DMA,
        ],
        compiler_params=pltpu.CompilerParams(vmem_limit_bytes=62 * MIB),
        cost_estimate=pl.CostEstimate(
            flops=16 * length * depth * wide, bytes_accessed=4 * depth * (length + 2 * wide), transcendentals=0
        ),
        name="project",
    )(place, x, *arrays)


def pack(columns):
    n = columns[0].shape[0]
    lane = lax.broadcasted_iota(jnp.int32, (n, 128), 1)
    full = jnp.zeros((n, 128), F32)
    for i, column in enumerate(columns):
        full = jnp.where(lane == i, column, full)
    full = full.T
    rows = [full[i : i + 1, j : j + 128] for i in range(len(columns)) for j in range(0, n, 128)]
    return jnp.broadcast_to(jnp.concatenate(rows, axis=0)[None], (16, len(rows), 128))


def unpack(got, count):
    total = jnp.sum(got, axis=0)
    rows = total.shape[0]
    full = jnp.concatenate([total, jnp.zeros((128 - rows, 128), F32)], axis=0).T
    each = rows // count
    return [
        jnp.concatenate([full[:, i * each + j : i * each + j + 1] for j in range(each)], axis=0) for i in range(count)
    ]


def merge_kernel(one, two, qkd, value, stats, *, wide):
    whole = [one[:, i * wide : (i + 1) * wide] + two[:, i * wide : (i + 1) * wide] for i in range(4)]
    for i in range(3):
        qkd[:, i * wide : (i + 1) * wide] = whole[i]
    value[...] = whole[3].astype(BF)
    q, key, dq = whole[:3]
    stats[...] = pack([jnp.sum(t, axis=1, keepdims=True) for t in (q * q, key * key, q * dq)])


def merge(one, two, wide):
    length = one.shape[0]
    return pl.pallas_call(
        functools.partial(merge_kernel, wide=wide),
        out_shape=[
            jax.ShapeDtypeStruct((length, 3 * wide), F32),
            jax.ShapeDtypeStruct((length, wide), BF),
            jax.ShapeDtypeStruct((16, 3 * length // 128, 128), F32),
        ],
        compiler_params=pltpu.CompilerParams(vmem_limit_bytes=16 * MIB),
        name="merge",
    )(one, two)


def attend_kernel(sums, qkd, value, gains, weighted, stats, *, wide, total):
    length = qkd.shape[0]
    scale = 1.0 / HD**0.5
    rq, rk, tq = unpack(sums[...], 3)
    rq = lax.rsqrt(rq / total + EPS)
    rk = lax.rsqrt(rk / total + EPS)
    tq = tq / total
    causal = lax.broadcasted_iota(jnp.int32, (length, length), 1) <= lax.broadcasted_iota(
        jnp.int32, (length, length), 0
    )
    nt = (((1,), (1,)), ((), ()))
    back = jnp.zeros((length, 1), F32)
    for h in range(wide // HD):
        at = slice(h * HD, (h + 1) * HD)
        q = qkd[:, h * HD : (h + 1) * HD]
        key = qkd[:, wide + h * HD : wide + (h + 1) * HD]
        dq = qkd[:, 2 * wide + h * HD : 2 * wide + (h + 1) * HD]
        v = value[:, at]
        gq, gk = gains[0:1, at], gains[1:2, at]
        qn = (gq * q * rq).astype(BF)
        kn = (gk * key * rk).astype(BF)
        dqn = (gq * rq * (dq - q * rq * rq * tq)).astype(BF)
        scores = lax.dot_general(qn, kn, nt, preferred_element_type=F32) * scale
        scores = jnp.where(causal, scores, -jnp.inf)
        expo = jnp.exp(scores - jnp.max(scores, axis=1, keepdims=True))
        probs = expo / jnp.sum(expo, axis=1, keepdims=True)
        ds = lax.dot_general(dqn, kn, nt, preferred_element_type=F32) * scale
        dpb = (probs * (ds - jnp.sum(probs * ds, axis=1, keepdims=True))).astype(BF)
        upper = jnp.dot(dpb, v, preferred_element_type=F32).astype(BF)
        gp = lax.dot_general(upper, v, nt, preferred_element_type=F32)
        gs = (probs * (gp - jnp.sum(probs * gp, axis=1, keepdims=True))).astype(BF)
        w = gq * (jnp.dot(gs, kn, preferred_element_type=F32) * scale)
        weighted[:, at] = w
        back += jnp.sum(q * w, axis=1, keepdims=True)
    stats[...] = pack([back])


def attend(sums, qkd, value, gains, wide, total):
    length = qkd.shape[0]
    return pl.pallas_call(
        functools.partial(attend_kernel, wide=wide, total=total),
        out_shape=[
            jax.ShapeDtypeStruct((length, wide), F32),
            jax.ShapeDtypeStruct((16, length // 128, 128), F32),
        ],
        compiler_params=pltpu.CompilerParams(vmem_limit_bytes=16 * MIB),
        name="attend",
    )(sums, qkd, value, gains)


def grad_kernel(sums, back, q, weighted, gq, *, total):
    rq = lax.rsqrt(unpack(sums[...], 3)[0] / total + EPS)
    tb = unpack(back[...], 1)[0] / total
    gq[...] = (rq * weighted[...] - q[...] * rq * rq * rq * tb).astype(BF)


def grad(sums, back, qkd, weighted, total):
    length, wide = weighted.shape
    return pl.pallas_call(
        functools.partial(grad_kernel, total=total),
        grid=(1,),
        in_specs=[
            pl.BlockSpec(sums.shape, lambda k: (0, 0, 0)),
            pl.BlockSpec(back.shape, lambda k: (0, 0, 0)),
            pl.BlockSpec((length, wide), lambda k: (0, 0)),
            pl.BlockSpec((length, wide), lambda k: (0, 0)),
        ],
        out_specs=pl.BlockSpec((length, wide), lambda k: (0, 0)),
        out_shape=jax.ShapeDtypeStruct((length, wide), BF),
        name="grad",
    )(sums, back, qkd, weighted)


def outer_kernel(place, x, near, gq, gq_core, gq_near, gq_near_core, term):
    length = gq.shape[0]
    total = jnp.dot(x[0, :, :length], gq[...], preferred_element_type=F32)
    total += jnp.dot(x[0, :, length:], gq_core[...], preferred_element_type=F32)
    total += jnp.dot(near[:, :length], gq_near[...], preferred_element_type=F32)
    total += jnp.dot(near[:, length:], gq_near_core[...], preferred_element_type=F32)
    term[...] = total.astype(BF)


def outer(place, x, near, grads):
    rows, tokens = near.shape
    length, wide = grads[0].shape
    steps = 2
    block = rows // steps
    return pl.pallas_call(
        outer_kernel,
        grid_spec=pltpu.PrefetchScalarGridSpec(
            num_scalar_prefetch=1,
            grid=(steps,),
            in_specs=[
                pl.BlockSpec((1, block, tokens), lambda k, place: (lax.rem(place[0], 2), k, 0)),
                pl.BlockSpec((block, tokens), lambda k, place: (k, 0)),
            ]
            + [pl.BlockSpec((length, wide), lambda k, place: (0, 0))] * 4,
            out_specs=pl.BlockSpec((block, wide), lambda k, place: (k, 0)),
        ),
        out_shape=jax.ShapeDtypeStruct((rows, wide), BF),
        compiler_params=pltpu.CompilerParams(vmem_limit_bytes=62 * MIB),
        cost_estimate=pl.CostEstimate(flops=4 * rows * tokens * wide, bytes_accessed=4 * rows * tokens, transcendentals=0),
        name="outer",
    )(place, x.reshape(2, rows, tokens), near, *grads)


def to_all(value, axes):
    return lax.all_to_all(value, axes, 0, 0, tiled=True)


def on_device(inputs, w_query, w_key, w_value, tangent, gain_query, gain_key):
    wide = w_query.shape[1]
    total = HEADS * HD
    place = jnp.stack([lax.axis_index(Y), lax.axis_index("zl")]).astype(jnp.int32)
    core = lax.axis_index("c")
    tie = lax.optimization_barrier

    halves = inputs[0].T.reshape(2, inputs.shape[2] // 2, inputs.shape[1])
    kept = lax.dynamic_index_in_dim(halves, core, 0, keepdims=False)
    given = lax.dynamic_index_in_dim(halves, 1 - core, 0, keepdims=False)
    x = jnp.concatenate([kept, shift(given, "c", 1, 2)], axis=1)
    x = lax.all_gather(x, ("zh", "x"), axis=0, tiled=True)

    weights = jnp.stack([w_query, w_key, tangent, w_value])
    parts = weight_ring(weights, shift(weights, "zl", 1, 2))
    x, *last = tie((x, parts[-1][0], parts[-2][0]))
    parts[-1], parts[-2] = (last[0], *parts[-1][1:]), (last[1], *parts[-2][1:])

    own, theirs, near = project(place, x, parts, wide)
    theirs = shift(theirs, "c", 1, 2)
    near = shift(near, "yl", 1, 2)
    qkd, value, stats = merge(own, theirs, wide)
    gains, stats = tie((jnp.stack([gain_query, gain_key]), stats))
    sums = to_all(stats, ("x", "zh"))
    weighted, stats = attend(sums, qkd, value, gains, wide, total)
    gq = grad(sums, to_all(stats, ("x", "zh")), qkd, weighted, total)

    gq_near = shift(gq, "yl", 1, 2)
    gq_core = shift(gq, "c", 1, 2)
    term = outer(place, x, near, (gq, gq_core, gq_near, shift(gq_near, "c", 1, 2)))
    got = to_all(term.reshape(8, -1, wide), ("zl", "yh"))
    return jnp.sum(got.astype(F32), axis=0)


def solution(mesh):
    fine = Mesh(mesh.devices.reshape(4, 2, 2, 2, 4, 4), ("yh", "yl", "zl", "c", "x", "zh"))
    dp, tensor = ("yh", "yl", "zl", "c"), ("x", "zh")
    return jax.shard_map(
        on_device,
        mesh=fine,
        in_specs=(
            P(dp, None, tensor),
            P(dp, tensor),
            P(dp, tensor),
            P(dp, tensor),
            P(dp, tensor),
            P(tensor),
            P(tensor),
        ),
        out_specs=P(dp, tensor),
        check_vma=False,
    )
```

```python
import functools

import jax
import jax.numpy as jnp
from jax import lax
from jax.experimental import pallas as pl
from jax.experimental.pallas import tpu as pltpu
from jax.sharding import Mesh, PartitionSpec as P

HEADS = 32
HD = 128
EPS = 1e-06
BF = jnp.bfloat16
F32 = jnp.float32
Y = ("yh", "yl")
MIB = 1024 * 1024


def shift(value, axis, by, size):
    return lax.ppermute(value, axis, [(i, (i + by) % size) for i in range(size)])


def weight_ring(own, other):
    up, down = shift(own, Y, 1, 8), shift(own, Y, -1, 8)
    parts = [(own, 0, 4, 0, 0, 0), (other, 0, 4, 0, 1, 0), (up, 0, 4, 1, 0, 0), (down, 0, 4, 7, 0, 0)]
    up = shift(jnp.concatenate([up, other]), Y, 1, 8)
    down = shift(jnp.concatenate([other, down]), Y, -1, 8)
    parts += [(up, 0, 4, 2, 0, 0), (up, 4, 4, 1, 1, 0), (down, 0, 4, 7, 1, 0), (down, 4, 4, 6, 0, 0)]
    up, down = shift(up, Y, 1, 8), shift(down, Y, -1, 8)
    parts += [(up, 0, 4, 3, 0, 0), (up, 4, 4, 2, 1, 0), (down, 0, 4, 6, 1, 0), (down, 4, 4, 5, 0, 0)]
    up, down = shift(up[2:], Y, 1, 8), shift(down[:6], Y, -1, 8)
    parts += [(up, 0, 2, 4, 0, 2), (up, 2, 4, 3, 1, 0), (down, 0, 4, 5, 1, 0), (down, 4, 2, 4, 0, 0)]
    up, down = shift(up[4:], Y, 1, 8), shift(down[:2], Y, -1, 8)
    parts += [(up, 0, 2, 4, 1, 2), (down, 0, 2, 4, 1, 0)]
    return parts


def project_kernel(place, x_hbm, *refs, layout, wide, rows):
    count = max(entry[0] for entry in layout) + 1
    pieces = refs[:count]
    own, theirs, near, x, w, sem, out_sem = refs[count:]
    length = own.shape[0]
    y, zl = place[0], place[1]
    groups = sem.shape[0]
    span = x.shape[0] // groups
    spots = {}
    for _, _, _, back, step, _ in layout:
        spots.setdefault((back, step), len(spots))

    def source(back, step):
        return lax.rem(y + 8 - back, 8), lax.rem(zl + step, 2)

    def block(index):
        return pl.ds(pl.multiple_of(index * rows, rows), rows)

    for (back, step), spot in spots.items():
        far_y, far_zl = source(back, step)
        at = pl.ds(spot * rows, rows)
        group = spot * rows // span
        index = (lax.rem(far_y, 2) * 2 + far_zl) * 4 + lax.div(far_y, 2)
        pltpu.make_async_copy(x_hbm.at[block(index), :], x.at[at, :], sem.at[group, 0]).start()
        for piece, first, entries, b, s, weight in layout:
            if (b, s) == (back, step):
                pltpu.make_async_copy(
                    pieces[piece].at[pl.ds(first, entries)], w.at[pl.ds(weight, entries), at, :], sem.at[group, 1]
                ).start()
    for g in range(groups):
        at = pl.ds(g * span, span)
        pltpu.make_async_copy(x.at[at, :], x.at[at, :], sem.at[g, 0]).wait()
        for (back, step), spot in spots.items():
            if back % 2 and spot * rows // span == g:
                far_y, far_zl = source(back, step)
                pltpu.make_async_copy(
                    x.at[pl.ds(spot * rows, rows), :], near.at[block(far_zl * 4 + lax.div(far_y, 2)), :], out_sem
                ).start()
        pltpu.make_async_copy(w.at[:, at, :], w.at[:, at, :], sem.at[g, 1]).wait()
        for i in range(4):
            part = lax.dot_general(x[at, :], w[i, at, :], (((0,), (0,)), ((), ())), preferred_element_type=F32)
            cols = slice(i * wide, (i + 1) * wide)
            own[:, cols] = part[:length] if g == 0 else own[:, cols] + part[:length]
            theirs[:, cols] = part[length:] if g == 0 else theirs[:, cols] + part[length:]
    pltpu.make_async_copy(near, near, out_sem).wait()


def project(place, x, parts, wide):
    depth, length = x.shape[0], x.shape[1] // 2
    arrays = []
    layout = []
    for array, *rest in parts:
        known = [i for i, other in enumerate(arrays) if other is array]
        if not known:
            arrays.append(array)
        layout.append((known[0] if known else len(arrays) - 1, *rest))
    return pl.pallas_call(
        functools.partial(project_kernel, layout=tuple(layout), wide=wide, rows=depth // 16),
        in_specs=[pl.BlockSpec(memory_space=pltpu.SMEM)]
        + [pl.BlockSpec(memory_space=pl.ANY)] * (1 + len(arrays)),
        out_specs=[
            pl.BlockSpec(memory_space=pltpu.VMEM),
            pl.BlockSpec(memory_space=pltpu.VMEM),
            pl.BlockSpec(memory_space=pl.ANY),
        ],
        out_shape=[
            jax.ShapeDtypeStruct((length, 4 * wide), F32),
            jax.ShapeDtypeStruct((length, 4 * wide), F32),
            jax.ShapeDtypeStruct((depth // 2, 2 * length), BF),
        ],
        scratch_shapes=[
            pltpu.VMEM(x.shape, BF),
            pltpu.VMEM((4, depth, wide), BF),
            pltpu.SemaphoreType.DMA((2, 2)),
            pltpu.SemaphoreType.DMA,
        ],
        compiler_params=pltpu.CompilerParams(vmem_limit_bytes=62 * MIB),
        cost_estimate=pl.CostEstimate(
            flops=16 * length * depth * wide, bytes_accessed=4 * depth * (length + 2 * wide), transcendentals=0
        ),
        name="project",
    )(place, x, *arrays)


def pack(columns):
    n = columns[0].shape[0]
    lane = lax.broadcasted_iota(jnp.int32, (n, 128), 1)
    full = jnp.zeros((n, 128), F32)
    for i, column in enumerate(columns):
        full = jnp.where(lane == i, column, full)
    full = full.T
    rows = [full[i : i + 1, j : j + 128] for i in range(len(columns)) for j in range(0, n, 128)]
    return jnp.broadcast_to(jnp.concatenate(rows, axis=0)[None], (16, len(rows), 128))


def unpack(got, count):
    total = jnp.sum(got, axis=0)
    rows = total.shape[0]
    full = jnp.concatenate([total, jnp.zeros((128 - rows, 128), F32)], axis=0).T
    each = rows // count
    return [
        jnp.concatenate([full[:, i * each + j : i * each + j + 1] for j in range(each)], axis=0) for i in range(count)
    ]


def merge_kernel(one, two, qkd, value, stats, *, wide):
    whole = [one[:, i * wide : (i + 1) * wide] + two[:, i * wide : (i + 1) * wide] for i in range(4)]
    for i in range(3):
        qkd[:, i * wide : (i + 1) * wide] = whole[i]
    value[...] = whole[3].astype(BF)
    q, key, dq = whole[:3]
    stats[...] = pack([jnp.sum(t, axis=1, keepdims=True) for t in (q * q, key * key, q * dq)])


def merge(one, two, wide):
    length = one.shape[0]
    return pl.pallas_call(
        functools.partial(merge_kernel, wide=wide),
        out_shape=[
            jax.ShapeDtypeStruct((length, 3 * wide), F32),
            jax.ShapeDtypeStruct((length, wide), BF),
            jax.ShapeDtypeStruct((16, 3 * length // 128, 128), F32),
        ],
        compiler_params=pltpu.CompilerParams(vmem_limit_bytes=16 * MIB),
        name="merge",
    )(one, two)


def attend_kernel(sums, qkd, value, gains, weighted, stats, *, wide, total):
    length = qkd.shape[0]
    scale = 1.0 / HD**0.5
    rq, rk, tq = unpack(sums[...], 3)
    rq = lax.rsqrt(rq / total + EPS)
    rk = lax.rsqrt(rk / total + EPS)
    tq = tq / total
    causal = lax.broadcasted_iota(jnp.int32, (length, length), 1) <= lax.broadcasted_iota(
        jnp.int32, (length, length), 0
    )
    nt = (((1,), (1,)), ((), ()))
    back = jnp.zeros((length, 1), F32)
    for h in range(wide // HD):
        at = slice(h * HD, (h + 1) * HD)
        q = qkd[:, h * HD : (h + 1) * HD]
        key = qkd[:, wide + h * HD : wide + (h + 1) * HD]
        dq = qkd[:, 2 * wide + h * HD : 2 * wide + (h + 1) * HD]
        v = value[:, at]
        gq, gk = gains[0:1, at], gains[1:2, at]
        qn = (gq * q * rq).astype(BF)
        kn = (gk * key * rk).astype(BF)
        dqn = (gq * rq * (dq - q * rq * rq * tq)).astype(BF)
        scores = lax.dot_general(qn, kn, nt, preferred_element_type=F32) * scale
        scores = jnp.where(causal, scores, -jnp.inf)
        expo = jnp.exp(scores - jnp.max(scores, axis=1, keepdims=True))
        probs = expo / jnp.sum(expo, axis=1, keepdims=True)
        ds = lax.dot_general(dqn, kn, nt, preferred_element_type=F32) * scale
        dpb = (probs * (ds - jnp.sum(probs * ds, axis=1, keepdims=True))).astype(BF)
        upper = jnp.dot(dpb, v, preferred_element_type=F32).astype(BF)
        gp = lax.dot_general(upper, v, nt, preferred_element_type=F32)
        gs = (probs * (gp - jnp.sum(probs * gp, axis=1, keepdims=True))).astype(BF)
        w = gq * (jnp.dot(gs, kn, preferred_element_type=F32) * scale)
        weighted[:, at] = w
        back += jnp.sum(q * w, axis=1, keepdims=True)
    stats[...] = pack([back])


def attend(sums, qkd, value, gains, wide, total):
    length = qkd.shape[0]
    return pl.pallas_call(
        functools.partial(attend_kernel, wide=wide, total=total),
        out_shape=[
            jax.ShapeDtypeStruct((length, wide), F32),
            jax.ShapeDtypeStruct((16, length // 128, 128), F32),
        ],
        compiler_params=pltpu.CompilerParams(vmem_limit_bytes=16 * MIB),
        name="attend",
    )(sums, qkd, value, gains)


def grad_kernel(sums, back, q, weighted, gq, *, total):
    rq = lax.rsqrt(unpack(sums[...], 3)[0] / total + EPS)
    tb = unpack(back[...], 1)[0] / total
    gq[...] = (rq * weighted[...] - q[...] * rq * rq * rq * tb).astype(BF)


def grad(sums, back, qkd, weighted, total):
    length, wide = weighted.shape
    return pl.pallas_call(
        functools.partial(grad_kernel, total=total),
        grid=(1,),
        in_specs=[
            pl.BlockSpec(sums.shape, lambda k: (0, 0, 0)),
            pl.BlockSpec(back.shape, lambda k: (0, 0, 0)),
            pl.BlockSpec((length, wide), lambda k: (0, 0)),
            pl.BlockSpec((length, wide), lambda k: (0, 0)),
        ],
        out_specs=pl.BlockSpec((length, wide), lambda k: (0, 0)),
        out_shape=jax.ShapeDtypeStruct((length, wide), BF),
        name="grad",
    )(sums, back, qkd, weighted)


def outer_kernel(x, near, gq, gq_core, gq_near, gq_near_core, term):
    length = gq.shape[0]
    total = jnp.dot(x[:, :length], gq[...], preferred_element_type=F32)
    total += jnp.dot(x[:, length:], gq_core[...], preferred_element_type=F32)
    total += jnp.dot(near[:, :length], gq_near[...], preferred_element_type=F32)
    total += jnp.dot(near[:, length:], gq_near_core[...], preferred_element_type=F32)
    term[...] = total.astype(BF)


def outer(x, near, grads):
    rows, tokens = near.shape
    wide = grads[0].shape[1]
    return pl.pallas_call(
        outer_kernel,
        out_shape=jax.ShapeDtypeStruct((rows, wide), BF),
        compiler_params=pltpu.CompilerParams(vmem_limit_bytes=16 * MIB),
        cost_estimate=pl.CostEstimate(flops=4 * rows * tokens * wide, bytes_accessed=4 * rows * tokens, transcendentals=0),
        name="outer",
    )(x, near, *grads)


def to_all(value, axes):
    return lax.all_to_all(value, axes, 0, 0, tiled=True)


def on_device(inputs, w_query, w_key, w_value, tangent, gain_query, gain_key):
    wide = w_query.shape[1]
    total = HEADS * HD
    place = jnp.stack([lax.axis_index(Y), lax.axis_index("zl")]).astype(jnp.int32)
    core = lax.axis_index("c")
    tie = lax.optimization_barrier

    halves = inputs[0].T.reshape(2, inputs.shape[2] // 2, inputs.shape[1])
    kept = lax.dynamic_index_in_dim(halves, core, 0, keepdims=False)
    given = lax.dynamic_index_in_dim(halves, 1 - core, 0, keepdims=False)
    x = jnp.concatenate([kept, shift(given, "c", 1, 2)], axis=1)
    x = lax.all_gather(x, ("zh", "x"), axis=0, tiled=True)

    weights = jnp.stack([w_query, w_key, tangent, w_value])
    parts = weight_ring(weights, shift(weights, "zl", 1, 2))
    x, *last = tie((x, parts[-1][0], parts[-2][0]))
    parts[-1], parts[-2] = (last[0], *parts[-1][1:]), (last[1], *parts[-2][1:])

    own, theirs, near = project(place, x, parts, wide)
    theirs = shift(theirs, "c", 1, 2)
    near = shift(near, "yl", 1, 2)
    qkd, value, stats = merge(own, theirs, wide)
    gains, stats = tie((jnp.stack([gain_query, gain_key]), stats))
    sums = to_all(stats, ("x", "zh"))
    weighted, stats = attend(sums, qkd, value, gains, wide, total)
    gq = grad(sums, to_all(stats, ("x", "zh")), qkd, weighted, total)

    gq_near = shift(gq, "yl", 1, 2)
    gq_core = shift(gq, "c", 1, 2)
    halves, gq = tie((x.reshape(2, -1, x.shape[1]), gq))
    mine = lax.dynamic_index_in_dim(halves, lax.axis_index("yl"), 0, keepdims=False)
    term = outer(mine, near, (gq, gq_core, gq_near, shift(gq_near, "c", 1, 2)))
    got = to_all(term.reshape(8, -1, wide), ("zl", "yh"))
    return jnp.sum(got.astype(F32), axis=0)


def solution(mesh):
    fine = Mesh(mesh.devices.reshape(4, 2, 2, 2, 4, 4), ("yh", "yl", "zl", "c", "x", "zh"))
    dp, tensor = ("yh", "yl", "zl", "c"), ("x", "zh")
    return jax.shard_map(
        on_device,
        mesh=fine,
        in_specs=(
            P(dp, None, tensor),
            P(dp, tensor),
            P(dp, tensor),
            P(dp, tensor),
            P(dp, tensor),
            P(tensor),
            P(tensor),
        ),
        out_specs=P(dp, tensor),
        check_vma=False,
    )
```

```python
import functools

import jax
import jax.numpy as jnp
from jax import lax
from jax.experimental import pallas as pl
from jax.experimental.pallas import tpu as pltpu
from jax.sharding import Mesh, PartitionSpec as P

HEADS = 32
HD = 128
EPS = 1e-06
BF = jnp.bfloat16
F32 = jnp.float32
Y = ("yh", "yl")
MIB = 1024 * 1024


def shift(value, axis, by, size):
    return lax.ppermute(value, axis, [(i, (i + by) % size) for i in range(size)])


def weight_ring(own, other):
    up, down = shift(own, Y, 1, 8), shift(own, Y, -1, 8)
    parts = [(own, 0, 4, 0, 0, 0), (other, 0, 4, 0, 1, 0), (up, 0, 4, 1, 0, 0), (down, 0, 4, 7, 0, 0)]
    up = shift(jnp.concatenate([up, other]), Y, 1, 8)
    down = shift(jnp.concatenate([other, down]), Y, -1, 8)
    parts += [(up, 0, 4, 2, 0, 0), (up, 4, 4, 1, 1, 0), (down, 0, 4, 7, 1, 0), (down, 4, 4, 6, 0, 0)]
    up, down = shift(up, Y, 1, 8), shift(down, Y, -1, 8)
    parts += [(up, 0, 4, 3, 0, 0), (up, 4, 4, 2, 1, 0), (down, 0, 4, 6, 1, 0), (down, 4, 4, 5, 0, 0)]
    up, down = shift(up[2:], Y, 1, 8), shift(down[:6], Y, -1, 8)
    parts += [(up, 0, 2, 4, 0, 2), (up, 2, 4, 3, 1, 0), (down, 0, 4, 5, 1, 0), (down, 4, 2, 4, 0, 0)]
    up, down = shift(up[4:], Y, 1, 8), shift(down[:2], Y, -1, 8)
    parts += [(up, 0, 2, 4, 1, 2), (down, 0, 2, 4, 1, 0)]
    return parts


def project_kernel(place, x_hbm, *refs, layout, wide, rows):
    count = max(entry[0] for entry in layout) + 1
    pieces = refs[:count]
    own, theirs, near, x, w, sem, out_sem = refs[count:]
    length = own.shape[0]
    y, zl = place[0], place[1]
    groups = sem.shape[0]
    span = x.shape[0] // groups
    spots = {}
    for _, _, _, back, step, _ in layout:
        spots.setdefault((back, step), len(spots))

    def source(back, step):
        return lax.rem(y + 8 - back, 8), lax.rem(zl + step, 2)

    def block(index):
        return pl.ds(pl.multiple_of(index * rows, rows), rows)

    for (back, step), spot in spots.items():
        far_y, far_zl = source(back, step)
        at = pl.ds(spot * rows, rows)
        group = spot * rows // span
        index = (lax.rem(far_y, 2) * 2 + far_zl) * 4 + lax.div(far_y, 2)
        pltpu.make_async_copy(x_hbm.at[block(index), :], x.at[at, :], sem.at[group, 0]).start()
        for piece, first, entries, b, s, weight in layout:
            if (b, s) == (back, step):
                pltpu.make_async_copy(
                    pieces[piece].at[pl.ds(first, entries)], w.at[pl.ds(weight, entries), at, :], sem.at[group, 1]
                ).start()
    for g in range(groups):
        at = pl.ds(g * span, span)
        pltpu.make_async_copy(x.at[at, :], x.at[at, :], sem.at[g, 0]).wait()
        for (back, step), spot in spots.items():
            if back % 2 and spot * rows // span == g:
                far_y, far_zl = source(back, step)
                pltpu.make_async_copy(
                    x.at[pl.ds(spot * rows, rows), :], near.at[block(far_zl * 4 + lax.div(far_y, 2)), :], out_sem
                ).start()
        pltpu.make_async_copy(w.at[:, at, :], w.at[:, at, :], sem.at[g, 1]).wait()
        for i in range(4):
            part = lax.dot_general(x[at, :], w[i, at, :], (((0,), (0,)), ((), ())), preferred_element_type=F32)
            cols = slice(i * wide, (i + 1) * wide)
            own[:, cols] = part[:length] if g == 0 else own[:, cols] + part[:length]
            theirs[:, cols] = part[length:] if g == 0 else theirs[:, cols] + part[length:]
    pltpu.make_async_copy(near, near, out_sem).wait()


def project(place, x, parts, wide):
    depth, length = x.shape[0], x.shape[1] // 2
    arrays = []
    layout = []
    for array, *rest in parts:
        known = [i for i, other in enumerate(arrays) if other is array]
        if not known:
            arrays.append(array)
        layout.append((known[0] if known else len(arrays) - 1, *rest))
    return pl.pallas_call(
        functools.partial(project_kernel, layout=tuple(layout), wide=wide, rows=depth // 16),
        in_specs=[pl.BlockSpec(memory_space=pltpu.SMEM)]
        + [pl.BlockSpec(memory_space=pl.ANY)] * (1 + len(arrays)),
        out_specs=[
            pl.BlockSpec(memory_space=pltpu.VMEM),
            pl.BlockSpec(memory_space=pltpu.VMEM),
            pl.BlockSpec(memory_space=pl.ANY),
        ],
        out_shape=[
            jax.ShapeDtypeStruct((length, 4 * wide), F32),
            jax.ShapeDtypeStruct((length, 4 * wide), F32),
            jax.ShapeDtypeStruct((depth // 2, 2 * length), BF),
        ],
        scratch_shapes=[
            pltpu.VMEM(x.shape, BF),
            pltpu.VMEM((4, depth, wide), BF),
            pltpu.SemaphoreType.DMA((2, 2)),
            pltpu.SemaphoreType.DMA,
        ],
        compiler_params=pltpu.CompilerParams(vmem_limit_bytes=62 * MIB),
        cost_estimate=pl.CostEstimate(
            flops=16 * length * depth * wide, bytes_accessed=4 * depth * (length + 2 * wide), transcendentals=0
        ),
        name="project",
    )(place, x, *arrays)


def pack(columns):
    n = columns[0].shape[0]
    lane = lax.broadcasted_iota(jnp.int32, (n, 128), 1)
    full = jnp.zeros((n, 128), F32)
    for i, column in enumerate(columns):
        full = jnp.where(lane == i, column, full)
    full = full.T
    row = jnp.concatenate([full[i : i + 1] for i in range(len(columns))], axis=1)
    return jnp.broadcast_to(row[None], (16, 1, row.shape[1]))


def unpack(got, count):
    total = jnp.sum(got, axis=0)
    rows = total.shape[1] // 128
    pieces = [total[:, j * 128 : (j + 1) * 128] for j in range(rows)]
    full = jnp.concatenate([*pieces, jnp.zeros((128 - rows, 128), F32)], axis=0).T
    each = rows // count
    return [
        jnp.concatenate([full[:, i * each + j : i * each + j + 1] for j in range(each)], axis=0) for i in range(count)
    ]


def merge_kernel(one, two, qkd, value, stats, *, wide):
    whole = [one[:, i * wide : (i + 1) * wide] + two[:, i * wide : (i + 1) * wide] for i in range(4)]
    for i in range(3):
        qkd[:, i * wide : (i + 1) * wide] = whole[i]
    value[...] = whole[3].astype(BF)
    q, key, dq = whole[:3]
    stats[...] = pack([jnp.sum(t, axis=1, keepdims=True) for t in (q * q, key * key, q * dq)])


def merge(one, two, wide):
    length = one.shape[0]
    return pl.pallas_call(
        functools.partial(merge_kernel, wide=wide),
        out_shape=[
            jax.ShapeDtypeStruct((length, 3 * wide), F32),
            jax.ShapeDtypeStruct((length, wide), BF),
            jax.ShapeDtypeStruct((16, 1, 3 * length), F32),
        ],
        compiler_params=pltpu.CompilerParams(vmem_limit_bytes=16 * MIB),
        name="merge",
    )(one, two)


def attend_kernel(sums, qkd, value, gains, weighted, stats, *, wide, total):
    length = qkd.shape[0]
    scale = 1.0 / HD**0.5
    rq, rk, tq = unpack(sums[...], 3)
    rq = lax.rsqrt(rq / total + EPS)
    rk = lax.rsqrt(rk / total + EPS)
    tq = tq / total
    causal = lax.broadcasted_iota(jnp.int32, (length, length), 1) <= lax.broadcasted_iota(
        jnp.int32, (length, length), 0
    )
    nt = (((1,), (1,)), ((), ()))
    back = jnp.zeros((length, 1), F32)
    for h in range(wide // HD):
        at = slice(h * HD, (h + 1) * HD)
        q = qkd[:, h * HD : (h + 1) * HD]
        key = qkd[:, wide + h * HD : wide + (h + 1) * HD]
        dq = qkd[:, 2 * wide + h * HD : 2 * wide + (h + 1) * HD]
        v = value[:, at]
        gq, gk = gains[0:1, at], gains[1:2, at]
        qn = (gq * q * rq).astype(BF)
        kn = (gk * key * rk).astype(BF)
        dqn = (gq * rq * (dq - q * rq * rq * tq)).astype(BF)
        scores = lax.dot_general(qn, kn, nt, preferred_element_type=F32) * scale
        scores = jnp.where(causal, scores, -jnp.inf)
        expo = jnp.exp(scores - jnp.max(scores, axis=1, keepdims=True))
        probs = expo / jnp.sum(expo, axis=1, keepdims=True)
        ds = lax.dot_general(dqn, kn, nt, preferred_element_type=F32) * scale
        dpb = (probs * (ds - jnp.sum(probs * ds, axis=1, keepdims=True))).astype(BF)
        upper = jnp.dot(dpb, v, preferred_element_type=F32).astype(BF)
        gp = lax.dot_general(upper, v, nt, preferred_element_type=F32)
        gs = (probs * (gp - jnp.sum(probs * gp, axis=1, keepdims=True))).astype(BF)
        w = gq * (jnp.dot(gs, kn, preferred_element_type=F32) * scale)
        weighted[:, at] = w
        back += jnp.sum(q * w, axis=1, keepdims=True)
    stats[...] = pack([back])


def attend(sums, qkd, value, gains, wide, total):
    length = qkd.shape[0]
    return pl.pallas_call(
        functools.partial(attend_kernel, wide=wide, total=total),
        out_shape=[
            jax.ShapeDtypeStruct((length, wide), F32),
            jax.ShapeDtypeStruct((16, 1, length), F32),
        ],
        compiler_params=pltpu.CompilerParams(vmem_limit_bytes=16 * MIB),
        name="attend",
    )(sums, qkd, value, gains)


def grad_kernel(sums, back, q, weighted, gq, *, total):
    rq = lax.rsqrt(unpack(sums[...], 3)[0] / total + EPS)
    tb = unpack(back[...], 1)[0] / total
    gq[...] = (rq * weighted[...] - q[...] * rq * rq * rq * tb).astype(BF)


def grad(sums, back, qkd, weighted, total):
    length, wide = weighted.shape
    return pl.pallas_call(
        functools.partial(grad_kernel, total=total),
        grid=(1,),
        in_specs=[
            pl.BlockSpec(sums.shape, lambda k: (0, 0, 0)),
            pl.BlockSpec(back.shape, lambda k: (0, 0, 0)),
            pl.BlockSpec((length, wide), lambda k: (0, 0)),
            pl.BlockSpec((length, wide), lambda k: (0, 0)),
        ],
        out_specs=pl.BlockSpec((length, wide), lambda k: (0, 0)),
        out_shape=jax.ShapeDtypeStruct((length, wide), BF),
        name="grad",
    )(sums, back, qkd, weighted)


def outer_kernel(x, near, gq, gq_core, gq_near, gq_near_core, term):
    length = gq.shape[0]
    total = jnp.dot(x[:, :length], gq[...], preferred_element_type=F32)
    total += jnp.dot(x[:, length:], gq_core[...], preferred_element_type=F32)
    total += jnp.dot(near[:, :length], gq_near[...], preferred_element_type=F32)
    total += jnp.dot(near[:, length:], gq_near_core[...], preferred_element_type=F32)
    term[...] = total.astype(BF)


def outer(x, near, grads):
    rows, tokens = near.shape
    wide = grads[0].shape[1]
    return pl.pallas_call(
        outer_kernel,
        out_shape=jax.ShapeDtypeStruct((rows, wide), BF),
        compiler_params=pltpu.CompilerParams(vmem_limit_bytes=16 * MIB),
        cost_estimate=pl.CostEstimate(flops=4 * rows * tokens * wide, bytes_accessed=4 * rows * tokens, transcendentals=0),
        name="outer",
    )(x, near, *grads)


def to_all(value, axes):
    return lax.all_to_all(value, axes, 0, 0, tiled=True)


def on_device(inputs, w_query, w_key, w_value, tangent, gain_query, gain_key):
    wide = w_query.shape[1]
    total = HEADS * HD
    place = jnp.stack([lax.axis_index(Y), lax.axis_index("zl")]).astype(jnp.int32)
    core = lax.axis_index("c")
    tie = lax.optimization_barrier

    halves = inputs[0].T.reshape(2, inputs.shape[2] // 2, inputs.shape[1])
    kept = lax.dynamic_index_in_dim(halves, core, 0, keepdims=False)
    given = lax.dynamic_index_in_dim(halves, 1 - core, 0, keepdims=False)
    x = jnp.concatenate([kept, shift(given, "c", 1, 2)], axis=1)
    x = lax.all_gather(x, ("zh", "x"), axis=0, tiled=True)

    weights = jnp.stack([w_query, w_key, tangent, w_value])
    parts = weight_ring(weights, shift(weights, "zl", 1, 2))
    x, *last = tie((x, parts[-1][0], parts[-2][0]))
    parts[-1], parts[-2] = (last[0], *parts[-1][1:]), (last[1], *parts[-2][1:])

    own, theirs, near = project(place, x, parts, wide)
    theirs = shift(theirs, "c", 1, 2)
    near = shift(near, "yl", 1, 2)
    qkd, value, stats = merge(own, theirs, wide)
    gains, stats = tie((jnp.stack([gain_query, gain_key]), stats))
    sums = to_all(stats, ("x", "zh"))
    weighted, stats = attend(sums, qkd, value, gains, wide, total)
    gq = grad(sums, to_all(stats, ("x", "zh")), qkd, weighted, total)

    gq_near = shift(gq, "yl", 1, 2)
    gq_core = shift(gq, "c", 1, 2)
    halves, gq = tie((x.reshape(2, -1, x.shape[1]), gq))
    mine = lax.dynamic_index_in_dim(halves, lax.axis_index("yl"), 0, keepdims=False)
    term = outer(mine, near, (gq, gq_core, gq_near, shift(gq_near, "c", 1, 2)))
    got = to_all(term.reshape(8, -1, wide), ("zl", "yh"))
    return jnp.sum(got.astype(F32), axis=0)


def solution(mesh):
    fine = Mesh(mesh.devices.reshape(4, 2, 2, 2, 4, 4), ("yh", "yl", "zl", "c", "x", "zh"))
    dp, tensor = ("yh", "yl", "zl", "c"), ("x", "zh")
    return jax.shard_map(
        on_device,
        mesh=fine,
        in_specs=(
            P(dp, None, tensor),
            P(dp, tensor),
            P(dp, tensor),
            P(dp, tensor),
            P(dp, tensor),
            P(tensor),
            P(tensor),
        ),
        out_specs=P(dp, tensor),
        check_vma=False,
    )
```

```python
import functools

import jax
import jax.numpy as jnp
from jax import lax
from jax.experimental import pallas as pl
from jax.experimental.pallas import tpu as pltpu
from jax.sharding import Mesh, PartitionSpec as P

HEADS = 32
HD = 128
EPS = 1e-06
BF = jnp.bfloat16
F32 = jnp.float32
Y = ("yh", "yl")
MIB = 1024 * 1024


def shift(value, axis, by, size):
    return lax.ppermute(value, axis, [(i, (i + by) % size) for i in range(size)])


def weight_ring(own, other):
    up, down = shift(own, Y, 1, 8), shift(own, Y, -1, 8)
    parts = [(own, 0, 4, 0, 0, 0), (other, 0, 4, 0, 1, 0), (up, 0, 4, 1, 0, 0), (down, 0, 4, 7, 0, 0)]
    up = shift(jnp.concatenate([up, other]), Y, 1, 8)
    down = shift(jnp.concatenate([other, down]), Y, -1, 8)
    parts += [(up, 0, 4, 2, 0, 0), (up, 4, 4, 1, 1, 0), (down, 0, 4, 7, 1, 0), (down, 4, 4, 6, 0, 0)]
    up, down = shift(up, Y, 1, 8), shift(down, Y, -1, 8)
    parts += [(up, 0, 4, 3, 0, 0), (up, 4, 4, 2, 1, 0), (down, 0, 4, 6, 1, 0), (down, 4, 4, 5, 0, 0)]
    up, down = shift(up[2:], Y, 1, 8), shift(down[:6], Y, -1, 8)
    parts += [(up, 0, 2, 4, 0, 2), (up, 2, 4, 3, 1, 0), (down, 0, 4, 5, 1, 0), (down, 4, 2, 4, 0, 0)]
    up, down = shift(up[4:], Y, 1, 8), shift(down[:2], Y, -1, 8)
    parts += [(up, 0, 2, 4, 1, 2), (down, 0, 2, 4, 1, 0)]
    return parts


def project_kernel(place, x_hbm, *refs, layout, wide, rows):
    count = max(entry[0] for entry in layout) + 1
    pieces = refs[:count]
    own, theirs, up, down, x, w, sem, out_sem = refs[count:]
    length = own.shape[0]
    y, zl = place[0], place[1]
    groups = sem.shape[0]
    span = x.shape[0] // groups
    spots = {}
    for _, _, _, back, step, _ in layout:
        spots.setdefault((back, step), len(spots))

    def source(back, step):
        return lax.rem(y + 8 - back, 8), lax.rem(zl + step, 2)

    def block(index):
        return pl.ds(pl.multiple_of(index * rows, rows), rows)

    for (back, step), spot in spots.items():
        far_y, far_zl = source(back, step)
        at = pl.ds(spot * rows, rows)
        group = spot * rows // span
        index = (lax.rem(far_y, 2) * 2 + far_zl) * 4 + lax.div(far_y, 2)
        pltpu.make_async_copy(x_hbm.at[block(index), :], x.at[at, :], sem.at[group, 0]).start()
        for piece, first, entries, b, s, weight in layout:
            if (b, s) == (back, step):
                pltpu.make_async_copy(
                    pieces[piece].at[pl.ds(first, entries)], w.at[pl.ds(weight, entries), at, :], sem.at[group, 1]
                ).start()
    for g in range(groups):
        at = pl.ds(g * span, span)
        pltpu.make_async_copy(x.at[at, :], x.at[at, :], sem.at[g, 0]).wait()
        for (back, step), spot in spots.items():
            if back % 2 and spot * rows // span == g:
                far_y, _ = source(back, step)
                pltpu.make_async_copy(
                    x.at[pl.ds(spot * rows, rows), :], (up, down)[step].at[block(lax.div(far_y, 2)), :], out_sem.at[step]
                ).start()
        pltpu.make_async_copy(w.at[:, at, :], w.at[:, at, :], sem.at[g, 1]).wait()
        for i in range(4):
            part = lax.dot_general(x[at, :], w[i, at, :], (((0,), (0,)), ((), ())), preferred_element_type=F32)
            cols = slice(i * wide, (i + 1) * wide)
            own[:, cols] = part[:length] if g == 0 else own[:, cols] + part[:length]
            theirs[:, cols] = part[length:] if g == 0 else theirs[:, cols] + part[length:]
    pltpu.make_async_copy(up, up, out_sem.at[0]).wait()
    pltpu.make_async_copy(down, down, out_sem.at[1]).wait()


def project(place, x, parts, wide):
    depth, length = x.shape[0], x.shape[1] // 2
    arrays = []
    layout = []
    for array, *rest in parts:
        known = [i for i, other in enumerate(arrays) if other is array]
        if not known:
            arrays.append(array)
        layout.append((known[0] if known else len(arrays) - 1, *rest))
    return pl.pallas_call(
        functools.partial(project_kernel, layout=tuple(layout), wide=wide, rows=depth // 16),
        in_specs=[pl.BlockSpec(memory_space=pltpu.SMEM)]
        + [pl.BlockSpec(memory_space=pl.ANY)] * (1 + len(arrays)),
        out_specs=[
            pl.BlockSpec(memory_space=pltpu.VMEM),
            pl.BlockSpec(memory_space=pltpu.VMEM),
            pl.BlockSpec(memory_space=pl.ANY),
            pl.BlockSpec(memory_space=pl.ANY),
        ],
        out_shape=[
            jax.ShapeDtypeStruct((length, 4 * wide), F32),
            jax.ShapeDtypeStruct((length, 4 * wide), F32),
            jax.ShapeDtypeStruct((depth // 4, 2 * length), BF),
            jax.ShapeDtypeStruct((depth // 4, 2 * length), BF),
        ],
        scratch_shapes=[
            pltpu.VMEM(x.shape, BF),
            pltpu.VMEM((4, depth, wide), BF),
            pltpu.SemaphoreType.DMA((2, 2)),
            pltpu.SemaphoreType.DMA((2,)),
        ],
        compiler_params=pltpu.CompilerParams(vmem_limit_bytes=62 * MIB),
        cost_estimate=pl.CostEstimate(
            flops=16 * length * depth * wide, bytes_accessed=4 * depth * (length + 2 * wide), transcendentals=0
        ),
        name="project",
    )(place, x, *arrays)


def pack(columns):
    n = columns[0].shape[0]
    lane = lax.broadcasted_iota(jnp.int32, (n, 128), 1)
    full = jnp.zeros((n, 128), F32)
    for i, column in enumerate(columns):
        full = jnp.where(lane == i, column, full)
    full = full.T
    row = jnp.concatenate([full[i : i + 1] for i in range(len(columns))], axis=1)
    return jnp.broadcast_to(row[None], (16, 1, row.shape[1]))


def unpack(got, count):
    total = jnp.sum(got, axis=0)
    rows = total.shape[1] // 128
    pieces = [total[:, j * 128 : (j + 1) * 128] for j in range(rows)]
    full = jnp.concatenate([*pieces, jnp.zeros((128 - rows, 128), F32)], axis=0).T
    each = rows // count
    return [
        jnp.concatenate([full[:, i * each + j : i * each + j + 1] for j in range(each)], axis=0) for i in range(count)
    ]


def merge_kernel(one, two, qkd, value, stats, *, wide):
    whole = [one[:, i * wide : (i + 1) * wide] + two[:, i * wide : (i + 1) * wide] for i in range(4)]
    for i in range(3):
        qkd[:, i * wide : (i + 1) * wide] = whole[i]
    value[...] = whole[3].astype(BF)
    q, key, dq = whole[:3]
    stats[...] = pack([jnp.sum(t, axis=1, keepdims=True) for t in (q * q, key * key, q * dq)])


def merge(one, two, wide):
    length = one.shape[0]
    return pl.pallas_call(
        functools.partial(merge_kernel, wide=wide),
        out_shape=[
            jax.ShapeDtypeStruct((length, 3 * wide), F32),
            jax.ShapeDtypeStruct((length, wide), BF),
            jax.ShapeDtypeStruct((16, 1, 3 * length), F32),
        ],
        compiler_params=pltpu.CompilerParams(vmem_limit_bytes=16 * MIB),
        name="merge",
    )(one, two)


def attend_kernel(sums, qkd, value, gains, weighted, stats, *, wide, total):
    length = qkd.shape[0]
    scale = 1.0 / HD**0.5
    rq, rk, tq = unpack(sums[...], 3)
    rq = lax.rsqrt(rq / total + EPS)
    rk = lax.rsqrt(rk / total + EPS)
    tq = tq / total
    causal = lax.broadcasted_iota(jnp.int32, (length, length), 1) <= lax.broadcasted_iota(
        jnp.int32, (length, length), 0
    )
    nt = (((1,), (1,)), ((), ()))
    back = jnp.zeros((length, 1), F32)
    for h in range(wide // HD):
        at = slice(h * HD, (h + 1) * HD)
        q = qkd[:, h * HD : (h + 1) * HD]
        key = qkd[:, wide + h * HD : wide + (h + 1) * HD]
        dq = qkd[:, 2 * wide + h * HD : 2 * wide + (h + 1) * HD]
        v = value[:, at]
        gq, gk = gains[0:1, at], gains[1:2, at]
        qn = (gq * q * rq).astype(BF)
        kn = (gk * key * rk).astype(BF)
        dqn = (gq * rq * (dq - q * rq * rq * tq)).astype(BF)
        scores = lax.dot_general(qn, kn, nt, preferred_element_type=F32) * scale
        scores = jnp.where(causal, scores, -jnp.inf)
        expo = jnp.exp(scores - jnp.max(scores, axis=1, keepdims=True))
        probs = expo / jnp.sum(expo, axis=1, keepdims=True)
        ds = lax.dot_general(dqn, kn, nt, preferred_element_type=F32) * scale
        dpb = (probs * (ds - jnp.sum(probs * ds, axis=1, keepdims=True))).astype(BF)
        upper = jnp.dot(dpb, v, preferred_element_type=F32).astype(BF)
        gp = lax.dot_general(upper, v, nt, preferred_element_type=F32)
        gs = (probs * (gp - jnp.sum(probs * gp, axis=1, keepdims=True))).astype(BF)
        w = gq * (jnp.dot(gs, kn, preferred_element_type=F32) * scale)
        weighted[:, at] = w
        back += jnp.sum(q * w, axis=1, keepdims=True)
    stats[...] = pack([back])


def attend(sums, qkd, value, gains, wide, total):
    length = qkd.shape[0]
    return pl.pallas_call(
        functools.partial(attend_kernel, wide=wide, total=total),
        out_shape=[
            jax.ShapeDtypeStruct((length, wide), F32),
            jax.ShapeDtypeStruct((16, 1, length), F32),
        ],
        compiler_params=pltpu.CompilerParams(vmem_limit_bytes=16 * MIB),
        name="attend",
    )(sums, qkd, value, gains)


def grad_kernel(sums, back, q, weighted, gq, *, total):
    rq = lax.rsqrt(unpack(sums[...], 3)[0] / total + EPS)
    tb = unpack(back[...], 1)[0] / total
    gq[...] = (rq * weighted[...] - q[...] * rq * rq * rq * tb).astype(BF)


def grad(sums, back, qkd, weighted, total):
    length, wide = weighted.shape
    return pl.pallas_call(
        functools.partial(grad_kernel, total=total),
        grid=(1,),
        in_specs=[
            pl.BlockSpec(sums.shape, lambda k: (0, 0, 0)),
            pl.BlockSpec(back.shape, lambda k: (0, 0, 0)),
            pl.BlockSpec((length, wide), lambda k: (0, 0)),
            pl.BlockSpec((length, wide), lambda k: (0, 0)),
        ],
        out_specs=pl.BlockSpec((length, wide), lambda k: (0, 0)),
        out_shape=jax.ShapeDtypeStruct((length, wide), BF),
        name="grad",
    )(sums, back, qkd, weighted)


def outer_kernel(place, x, up, down, gq, gq_core, gq_up, gq_down, gq_cores, term):
    length, half = gq.shape[0], up.shape[0]
    for step, (near, gq_near) in enumerate(((up, gq_up), (down, gq_down))):
        at = pl.ds(pl.multiple_of(lax.rem(place[1] + step, 2) * half, half), half)
        total = jnp.dot(x[at, :length], gq[...], preferred_element_type=F32)
        total += jnp.dot(x[at, length:], gq_core[...], preferred_element_type=F32)
        total += jnp.dot(near[:, :length], gq_near[...], preferred_element_type=F32)
        cores = gq_cores[step * length : (step + 1) * length, :]
        total += jnp.dot(near[:, length:], cores, preferred_element_type=F32)
        term[at, :] = total.astype(BF)


def outer(place, x, *rest):
    rows, tokens = x.shape
    wide = rest[2].shape[1]
    return pl.pallas_call(
        outer_kernel,
        in_specs=[pl.BlockSpec(memory_space=pltpu.SMEM)] + [pl.BlockSpec(memory_space=pltpu.VMEM)] * (1 + len(rest)),
        out_shape=jax.ShapeDtypeStruct((rows, wide), BF),
        compiler_params=pltpu.CompilerParams(vmem_limit_bytes=16 * MIB),
        cost_estimate=pl.CostEstimate(flops=4 * rows * tokens * wide, bytes_accessed=4 * rows * tokens, transcendentals=0),
        name="outer",
    )(place, x, *rest)


def to_all(value, axes):
    return lax.all_to_all(value, axes, 0, 0, tiled=True)


def on_device(inputs, w_query, w_key, w_value, tangent, gain_query, gain_key):
    wide = w_query.shape[1]
    total = HEADS * HD
    place = jnp.stack([lax.axis_index(Y), lax.axis_index("zl")]).astype(jnp.int32)
    core = lax.axis_index("c")
    tie = lax.optimization_barrier

    halves = inputs[0].T.reshape(2, inputs.shape[2] // 2, inputs.shape[1])
    kept = lax.dynamic_index_in_dim(halves, core, 0, keepdims=False)
    given = lax.dynamic_index_in_dim(halves, 1 - core, 0, keepdims=False)
    x = jnp.concatenate([kept, shift(given, "c", 1, 2)], axis=1)
    x = lax.all_gather(x, ("zh", "x"), axis=0, tiled=True)

    weights = jnp.stack([w_query, w_key, tangent, w_value])
    parts = weight_ring(weights, shift(weights, "zl", 1, 2))
    x, *last = tie((x, parts[-1][0], parts[-2][0]))
    parts[-1], parts[-2] = (last[0], *parts[-1][1:]), (last[1], *parts[-2][1:])

    own, theirs, up, down = project(place, x, parts, wide)
    theirs = shift(theirs, "c", 1, 2)
    up, down = shift(up, Y, 1, 8), shift(down, Y, -1, 8)
    qkd, value, stats = merge(own, theirs, wide)
    gains, stats = tie((jnp.stack([gain_query, gain_key]), stats))
    sums = to_all(stats, ("x", "zh"))
    weighted, stats = attend(sums, qkd, value, gains, wide, total)
    gq = grad(sums, to_all(stats, ("x", "zh")), qkd, weighted, total)

    gq_up, gq_down = shift(gq, Y, 1, 8), shift(gq, Y, -1, 8)
    gq_core = shift(gq, "c", 1, 2)
    halves, gq = tie((x.reshape(2, -1, x.shape[1]), gq))
    mine = lax.dynamic_index_in_dim(halves, lax.axis_index("yl"), 0, keepdims=False)
    gq_cores = shift(jnp.concatenate([gq_up, gq_down], axis=0), "c", 1, 2)
    term = outer(place, mine, up, down, gq, gq_core, gq_up, gq_down, gq_cores)
    got = to_all(term.reshape(8, -1, wide), ("zl", "yh"))
    return jnp.sum(got.astype(F32), axis=0)


def solution(mesh):
    fine = Mesh(mesh.devices.reshape(4, 2, 2, 2, 4, 4), ("yh", "yl", "zl", "c", "x", "zh"))
    dp, tensor = ("yh", "yl", "zl", "c"), ("x", "zh")
    return jax.shard_map(
        on_device,
        mesh=fine,
        in_specs=(
            P(dp, None, tensor),
            P(dp, tensor),
            P(dp, tensor),
            P(dp, tensor),
            P(dp, tensor),
            P(tensor),
            P(tensor),
        ),
        out_specs=P(dp, tensor),
        check_vma=False,
    )
```

```python
import functools

import jax
import jax.numpy as jnp
from jax import lax
from jax.experimental import pallas as pl
from jax.experimental.pallas import tpu as pltpu
from jax.sharding import Mesh, PartitionSpec as P

HEADS = 32
HD = 128
EPS = 1e-06
BF = jnp.bfloat16
F32 = jnp.float32
Y = ("yh", "yl")
MIB = 1024 * 1024


def shift(value, axis, by, size):
    return lax.ppermute(value, axis, [(i, (i + by) % size) for i in range(size)])


def weight_ring(own, other):
    up, down = shift(own, Y, 1, 8), shift(own, Y, -1, 8)
    parts = [(own, 0, 4, 0, 0, 0), (other, 0, 4, 0, 1, 0), (up, 0, 4, 1, 0, 0), (down, 0, 4, 7, 0, 0)]
    up = shift(jnp.concatenate([up, other]), Y, 1, 8)
    down = shift(jnp.concatenate([other, down]), Y, -1, 8)
    parts += [(up, 0, 4, 2, 0, 0), (up, 4, 4, 1, 1, 0), (down, 0, 4, 7, 1, 0), (down, 4, 4, 6, 0, 0)]
    up, down = shift(up, Y, 1, 8), shift(down, Y, -1, 8)
    parts += [(up, 0, 4, 3, 0, 0), (up, 4, 4, 2, 1, 0), (down, 0, 4, 6, 1, 0), (down, 4, 4, 5, 0, 0)]
    up, down = shift(up[2:], Y, 1, 8), shift(down[:6], Y, -1, 8)
    parts += [(up, 0, 2, 4, 0, 2), (up, 2, 4, 3, 1, 0), (down, 0, 4, 5, 1, 0), (down, 4, 2, 4, 0, 0)]
    up, down = shift(up[4:], Y, 1, 8), shift(down[:2], Y, -1, 8)
    parts += [(up, 0, 2, 4, 1, 2), (down, 0, 2, 4, 1, 0)]
    return parts


def project_kernel(place, x_hbm, *refs, layout, wide, rows):
    count = max(entry[0] for entry in layout) + 1
    pieces = refs[:count]
    own, theirs, near, x, w, sem, out_sem = refs[count:]
    length = own.shape[0]
    y, zl = place[0], place[1]
    groups = sem.shape[0]
    span = x.shape[0] // groups
    spots = {}
    for _, _, _, back, step, _ in layout:
        spots.setdefault((back, step), len(spots))

    def source(back, step):
        return lax.rem(y + 8 - back, 8), lax.rem(zl + step, 2)

    def block(index):
        return pl.ds(pl.multiple_of(index * rows, rows), rows)

    for (back, step), spot in spots.items():
        far_y, far_zl = source(back, step)
        at = pl.ds(spot * rows, rows)
        group = spot * rows // span
        index = (lax.rem(far_y, 2) * 2 + far_zl) * 4 + lax.div(far_y, 2)
        pltpu.make_async_copy(x_hbm.at[block(index), :], x.at[at, :], sem.at[group, 0]).start()
        for piece, first, entries, b, s, weight in layout:
            if (b, s) == (back, step):
                pltpu.make_async_copy(
                    pieces[piece].at[pl.ds(first, entries)], w.at[pl.ds(weight, entries), at, :], sem.at[group, 1]
                ).start()
    for g in range(groups):
        at = pl.ds(g * span, span)
        pltpu.make_async_copy(x.at[at, :], x.at[at, :], sem.at[g, 0]).wait()
        for (back, step), spot in spots.items():
            if back % 2 and spot * rows // span == g:
                far_y, far_zl = source(back, step)
                pltpu.make_async_copy(
                    x.at[pl.ds(spot * rows, rows), :], near.at[block(far_zl * 4 + lax.div(far_y, 2)), :], out_sem
                ).start()
        pltpu.make_async_copy(w.at[:, at, :], w.at[:, at, :], sem.at[g, 1]).wait()
        for i in range(4):
            part = lax.dot_general(x[at, :], w[i, at, :], (((0,), (0,)), ((), ())), preferred_element_type=F32)
            cols = slice(i * wide, (i + 1) * wide)
            own[:, cols] = part[:length] if g == 0 else own[:, cols] + part[:length]
            theirs[:, cols] = part[length:] if g == 0 else theirs[:, cols] + part[length:]
    pltpu.make_async_copy(near, near, out_sem).wait()


def project(place, x, parts, wide):
    depth, length = x.shape[0], x.shape[1] // 2
    arrays = []
    layout = []
    for array, *rest in parts:
        known = [i for i, other in enumerate(arrays) if other is array]
        if not known:
            arrays.append(array)
        layout.append((known[0] if known else len(arrays) - 1, *rest))
    return pl.pallas_call(
        functools.partial(project_kernel, layout=tuple(layout), wide=wide, rows=depth // 16),
        in_specs=[pl.BlockSpec(memory_space=pltpu.SMEM)]
        + [pl.BlockSpec(memory_space=pl.ANY)] * (1 + len(arrays)),
        out_specs=[
            pl.BlockSpec(memory_space=pltpu.VMEM),
            pl.BlockSpec(memory_space=pltpu.VMEM),
            pl.BlockSpec(memory_space=pl.ANY),
        ],
        out_shape=[
            jax.ShapeDtypeStruct((length, 4 * wide), F32),
            jax.ShapeDtypeStruct((length, 4 * wide), F32),
            jax.ShapeDtypeStruct((depth // 2, 2 * length), BF),
        ],
        scratch_shapes=[
            pltpu.VMEM(x.shape, BF),
            pltpu.VMEM((4, depth, wide), BF),
            pltpu.SemaphoreType.DMA((2, 2)),
            pltpu.SemaphoreType.DMA,
        ],
        compiler_params=pltpu.CompilerParams(vmem_limit_bytes=44 * MIB),
        cost_estimate=pl.CostEstimate(
            flops=16 * length * depth * wide, bytes_accessed=4 * depth * (length + 2 * wide), transcendentals=0
        ),
        name="project",
    )(place, x, *arrays)


def pack(columns):
    n = columns[0].shape[0]
    lane = lax.broadcasted_iota(jnp.int32, (n, 128), 1)
    full = jnp.zeros((n, 128), F32)
    for i, column in enumerate(columns):
        full = jnp.where(lane == i, column, full)
    full = full.T
    rows = [full[i : i + 1, j : j + 128] for i in range(len(columns)) for j in range(0, n, 128)]
    return jnp.broadcast_to(jnp.concatenate(rows, axis=0)[None], (16, len(rows), 128))


def unpack(got, count):
    total = jnp.sum(got, axis=0)
    rows = total.shape[0]
    full = jnp.concatenate([total, jnp.zeros((128 - rows, 128), F32)], axis=0).T
    each = rows // count
    return [
        jnp.concatenate([full[:, i * each + j : i * each + j + 1] for j in range(each)], axis=0) for i in range(count)
    ]


def merge_kernel(one, two, qkd, value, stats, *, wide):
    whole = [one[:, i * wide : (i + 1) * wide] + two[:, i * wide : (i + 1) * wide] for i in range(4)]
    for i in range(3):
        qkd[:, i * wide : (i + 1) * wide] = whole[i]
    value[...] = whole[3].astype(BF)
    q, key, dq = whole[:3]
    stats[...] = pack([jnp.sum(t, axis=1, keepdims=True) for t in (q * q, key * key, q * dq)])


def merge(one, two, wide):
    length = one.shape[0]
    return pl.pallas_call(
        functools.partial(merge_kernel, wide=wide),
        out_shape=[
            jax.ShapeDtypeStruct((length, 3 * wide), F32),
            jax.ShapeDtypeStruct((length, wide), BF),
            jax.ShapeDtypeStruct((16, 3 * length // 128, 128), F32),
        ],
        compiler_params=pltpu.CompilerParams(vmem_limit_bytes=16 * MIB),
        name="merge",
    )(one, two)


def attend_kernel(sums, qkd, value, gains, weighted, stats, *, wide, total):
    length = qkd.shape[0]
    scale = 1.0 / HD**0.5
    rq, rk, tq = unpack(sums[...], 3)
    rq = lax.rsqrt(rq / total + EPS)
    rk = lax.rsqrt(rk / total + EPS)
    tq = tq / total
    causal = lax.broadcasted_iota(jnp.int32, (length, length), 1) <= lax.broadcasted_iota(
        jnp.int32, (length, length), 0
    )
    nt = (((1,), (1,)), ((), ()))
    back = jnp.zeros((length, 1), F32)
    for h in range(wide // HD):
        at = slice(h * HD, (h + 1) * HD)
        q = qkd[:, h * HD : (h + 1) * HD]
        key = qkd[:, wide + h * HD : wide + (h + 1) * HD]
        dq = qkd[:, 2 * wide + h * HD : 2 * wide + (h + 1) * HD]
        v = value[:, at]
        gq, gk = gains[0:1, at], gains[1:2, at]
        qn = (gq * q * rq).astype(BF)
        kn = (gk * key * rk).astype(BF)
        dqn = (gq * rq * (dq - q * rq * rq * tq)).astype(BF)
        scores = lax.dot_general(qn, kn, nt, preferred_element_type=F32) * scale
        scores = jnp.where(causal, scores, -jnp.inf)
        expo = jnp.exp(scores - jnp.max(scores, axis=1, keepdims=True))
        probs = expo / jnp.sum(expo, axis=1, keepdims=True)
        ds = lax.dot_general(dqn, kn, nt, preferred_element_type=F32) * scale
        dpb = (probs * (ds - jnp.sum(probs * ds, axis=1, keepdims=True))).astype(BF)
        upper = jnp.dot(dpb, v, preferred_element_type=F32).astype(BF)
        gp = lax.dot_general(upper, v, nt, preferred_element_type=F32)
        gs = (probs * (gp - jnp.sum(probs * gp, axis=1, keepdims=True))).astype(BF)
        w = gq * (jnp.dot(gs, kn, preferred_element_type=F32) * scale)
        weighted[:, at] = w
        back += jnp.sum(q * w, axis=1, keepdims=True)
    stats[...] = pack([back])


def attend(sums, qkd, value, gains, wide, total):
    length = qkd.shape[0]
    return pl.pallas_call(
        functools.partial(attend_kernel, wide=wide, total=total),
        out_shape=[
            jax.ShapeDtypeStruct((length, wide), F32),
            jax.ShapeDtypeStruct((16, length // 128, 128), F32),
        ],
        compiler_params=pltpu.CompilerParams(vmem_limit_bytes=16 * MIB),
        name="attend",
    )(sums, qkd, value, gains)


def grad_kernel(sums, back, q, weighted, gq, *, total):
    rq = lax.rsqrt(unpack(sums[...], 3)[0] / total + EPS)
    tb = unpack(back[...], 1)[0] / total
    gq[...] = (rq * weighted[...] - q[...] * rq * rq * rq * tb).astype(BF)


def grad(sums, back, qkd, weighted, total):
    length, wide = weighted.shape
    return pl.pallas_call(
        functools.partial(grad_kernel, total=total),
        grid=(1,),
        in_specs=[
            pl.BlockSpec(sums.shape, lambda k: (0, 0, 0)),
            pl.BlockSpec(back.shape, lambda k: (0, 0, 0)),
            pl.BlockSpec((length, wide), lambda k: (0, 0)),
            pl.BlockSpec((length, wide), lambda k: (0, 0)),
        ],
        out_specs=pl.BlockSpec((length, wide), lambda k: (0, 0)),
        out_shape=jax.ShapeDtypeStruct((length, wide), BF),
        name="grad",
    )(sums, back, qkd, weighted)


def outer_kernel(x, near, gq, gq_core, gq_near, gq_near_core, term):
    length = gq.shape[0]
    total = jnp.dot(x[:, :length], gq[...], preferred_element_type=F32)
    total += jnp.dot(x[:, length:], gq_core[...], preferred_element_type=F32)
    total += jnp.dot(near[:, :length], gq_near[...], preferred_element_type=F32)
    total += jnp.dot(near[:, length:], gq_near_core[...], preferred_element_type=F32)
    term[...] = total.astype(BF)


def outer(x, near, grads):
    rows, tokens = near.shape
    wide = grads[0].shape[1]
    return pl.pallas_call(
        outer_kernel,
        out_shape=jax.ShapeDtypeStruct((rows, wide), BF),
        compiler_params=pltpu.CompilerParams(vmem_limit_bytes=16 * MIB),
        cost_estimate=pl.CostEstimate(flops=4 * rows * tokens * wide, bytes_accessed=4 * rows * tokens, transcendentals=0),
        name="outer",
    )(x, near, *grads)


def to_all(value, axes):
    return lax.all_to_all(value, axes, 0, 0, tiled=True)


def on_device(inputs, w_query, w_key, w_value, tangent, gain_query, gain_key):
    wide = w_query.shape[1]
    total = HEADS * HD
    place = jnp.stack([lax.axis_index(Y), lax.axis_index("zl")]).astype(jnp.int32)
    core = lax.axis_index("c")
    tie = lax.optimization_barrier

    halves = inputs[0].T.reshape(2, inputs.shape[2] // 2, inputs.shape[1])
    kept = lax.dynamic_index_in_dim(halves, core, 0, keepdims=False)
    given = lax.dynamic_index_in_dim(halves, 1 - core, 0, keepdims=False)
    x = jnp.concatenate([kept, shift(given, "c", 1, 2)], axis=1)
    x = lax.all_gather(x, ("zh", "x"), axis=0, tiled=True)

    weights = jnp.stack([w_query, w_key, tangent, w_value])
    parts = weight_ring(weights, shift(weights, "zl", 1, 2))
    x, *last = tie((x, parts[-1][0], parts[-2][0]))
    parts[-1], parts[-2] = (last[0], *parts[-1][1:]), (last[1], *parts[-2][1:])

    own, theirs, near = project(place, x, parts, wide)
    theirs = shift(theirs, "c", 1, 2)
    near = shift(near, "yl", 1, 2)
    qkd, value, stats = merge(own, theirs, wide)
    gains, stats = tie((jnp.stack([gain_query, gain_key]), stats))
    sums = to_all(stats, ("x", "zh"))
    weighted, stats = attend(sums, qkd, value, gains, wide, total)
    gq = grad(sums, to_all(stats, ("x", "zh")), qkd, weighted, total)

    gq_near = shift(gq, "yl", 1, 2)
    gq_core = shift(gq, "c", 1, 2)
    halves, gq = tie((x.reshape(2, -1, x.shape[1]), gq))
    mine = lax.dynamic_index_in_dim(halves, lax.axis_index("yl"), 0, keepdims=False)
    term = outer(mine, near, (gq, gq_core, gq_near, shift(gq_near, "c", 1, 2)))
    got = to_all(term.reshape(8, -1, wide), ("zl", "yh"))
    return jnp.sum(got.astype(F32), axis=0)


def solution(mesh):
    fine = Mesh(mesh.devices.reshape(4, 2, 2, 2, 4, 4), ("yh", "yl", "zl", "c", "x", "zh"))
    dp, tensor = ("yh", "yl", "zl", "c"), ("x", "zh")
    return jax.shard_map(
        on_device,
        mesh=fine,
        in_specs=(
            P(dp, None, tensor),
            P(dp, tensor),
            P(dp, tensor),
            P(dp, tensor),
            P(dp, tensor),
            P(tensor),
            P(tensor),
        ),
        out_specs=P(dp, tensor),
        check_vma=False,
    )
```
